256 devices in a mesh: gx: 32 (over y_lo, z, core), gy: 8 (over x, y_hi).
Axes of the slice: x: 4, y: 4 (y_hi: 2, y_lo: 2; y = y_hi * 2 + y_lo), z: 8, core: 2. Of those that a mesh axis runs over, the one named last changes fastest.
Arguments:
- offsets: float32 [3, 128, 320, 128], P(None, 'gx', 'gy'), may hold values from 0 to 16, as said below
- charges: float32 [128, 320, 128], P('gx', 'gy'), may hold values from -4 to 4
- atom_type: int32 [128, 320, 128], P('gx', 'gy'), may hold values from 0 to 15
- type_radius: float32 [16], replicated, may hold values from 1.2 to 2
- type_scale: float32 [16], replicated, may hold values from 0.5 to 0.85
- tile_mask: int32 [128, 320, 25], P('gx', 'gy'), may hold values from 0 to 1, as said below
Outputs:
- born_radius: float32 [128, 320, 128], P('gx', 'gy')
- atom_energy: float32 [128, 320, 128], P('gx', 'gy')
- force: float32 [3, 128, 320, 128], P(None, 'gx', 'gy')
- born_grad: float32 [128, 320, 128], P('gx', 'gy')
The draws below stay inside these ranges and needn't reach their ends.
Inputs may be any that keep to these rules, and one draw needn't show every extreme that they name: `offsets`: atoms of a block sit on a 4 x 4 x 128/16 lattice of spacing 2 starting at 1, each coordinate moved by at most 0.5; blocks are 8 wide in the first two dimensions. `tile_mask`: entry k of block (u, v) equals entry 24 - k of block (u + k // 5 - 2, v + k % 5 - 2), the grid wrapping in both dimensions, and entry 12 is always 1. In every draw all 160 blocks of some device have all 25 entries 1.
All inputs are finite; a program needn't handle non-finite values.
Results may differ from the reference program's by a relative error of at most 0.0003.
Values sent between devices are 32-bit elements; how exact they have to be, the bound alone decides.
A program may use at most 64 MiB of HBM per device.

```python
import math
import jax
import jax.numpy as jnp
from jax import lax

BX = 4
BY = 40
B = 128
NTYPES = 16
GBX = 128
GBY = 320


def draw_offsets(key, part):
    key = jax.random.fold_in(key, 5)
    first_key = jax.random.fold_in(key, 0)
    atom_index = jnp.arange(B, dtype=jnp.int32)
    lattice = jnp.stack([atom_index % 4, atom_index // 4 % 4, atom_index // 16]).astype(jnp.float32) * 2.0 + 1.0
    full_shape = (3, GBX, GBY, B)
    jitter = jax.random.uniform(first_key, full_shape, jnp.float32, -0.5, 0.5)
    return lattice[:, None, None, :] + jitter


def draw_tile_mask(key, part):
    key = jax.random.fold_in(key, 11)
    level_key, pick_key, bit_key = jax.random.split(key, 3)
    device_rows = GBX // BX
    device_cols = GBY // BY
    levels = jax.random.randint(level_key, (device_rows, device_cols), 10, 101)
    chance = jnp.repeat(jnp.repeat(levels * levels // 100, BX, axis=0), BY, axis=1)
    center = jax.random.randint(pick_key, (2,), 0, 1 << 30)
    center_x = center[0] % device_rows
    center_y = center[1] % device_cols
    block_x = jnp.arange(GBX, dtype=jnp.int32)[:, None]
    block_y = jnp.arange(GBY, dtype=jnp.int32)[None, :]
    near_x = (block_x - center_x * BX + 2) % GBX < BX + 4
    near_y = (block_y - center_y * BY + 2) % GBY < BY + 4
    chance = jnp.where(near_x & near_y, 100, chance)
    upper_bits = (jax.random.randint(bit_key, (GBX, GBY, 12), 0, 100) < chance[:, :, None]).astype(jnp.int32)
    columns = []
    for offset_code in range(25):
        step_x, step_y = (offset_code // 5 - 2, offset_code % 5 - 2)
        if offset_code < 12:
            columns.append(jnp.roll(upper_bits[:, :, 11 - offset_code], (-step_x, -step_y), axis=(0, 1)))
        elif offset_code == 12:
            columns.append(jnp.ones((GBX, GBY), jnp.int32))
        else:
            columns.append(upper_bits[:, :, offset_code - 13])
    return jnp.stack(columns, axis=-1)


def touch_ends(values, key, smallest, largest):
    longest = values.shape.index(max(values.shape))
    spots = []
    for shift in (0, 1):
        where = [jax.random.randint(jax.random.fold_in(key, axis), (), 0, length) for axis, length in enumerate(values.shape)]
        where[longest] = (where[longest] + shift) % values.shape[longest]
        spots.append(tuple(where))
    return values.at[spots[0]].set(smallest).at[spots[1]].set(largest)


def block_scale(own_key, shape, cuts, least, high):
    def one(position, shards_of):
        heights = jax.random.uniform(jax.random.fold_in(jax.random.fold_in(own_key, 6), position), (shards_of,), jnp.float32, least / len(cuts), high / len(cuts))
        return jnp.repeat(jnp.exp(heights), shape[position] // shards_of).reshape((-1,) + (1,) * (len(shape) - position - 1))

    gain = one(*cuts[0])
    for cut in cuts[1:]:
        gain = gain * one(*cut)
    return gain


def gaussian(rng, shape, scale, reach, pieces=(), held_as=jnp.bfloat16):
    values = jax.random.normal(rng, shape, jnp.float32) * scale
    if len(pieces) > 0:
        values = block_scale(rng, shape, pieces, -0.22, 0.18) * values
    return jnp.clip(values, min=-reach, max=reach).astype(held_as)


def setup_inputs(seed: int = 0) -> dict:
    arg_keys = jax.random.split(jax.random.key(seed), 7)
    return {
        "offsets": draw_offsets(jax.random.fold_in(arg_keys[6], 71), 0),
        "charges": gaussian(arg_keys[1], (GBX, GBY, B), 1.0, 4.0, ((0, 32), (1, 8)), jnp.float32),
        "atom_type": touch_ends(jax.random.randint(arg_keys[2], (GBX, GBY, B), 0, NTYPES), jax.random.fold_in(arg_keys[2], 1), 0, NTYPES - 1).astype(jnp.int32),
        "type_radius": jnp.clip(jnp.exp(jax.random.uniform(arg_keys[3], (NTYPES,), jnp.float32, math.log(1.2), math.log(2.0))), 1.2, 2.0),
        "type_scale": jnp.clip(jax.random.uniform(arg_keys[4], (NTYPES,), jnp.float32, 0.5, 0.85), 0.5, 0.85),
        "tile_mask": draw_tile_mask(jax.random.fold_in(arg_keys[6], 71), 0),
    }


dielectric_factor = 1.0 - 1.0 / 78.5
radius_offset = 0.09
block_side = 8.0

def atom_terms(atom_type, type_radius, type_scale):
    type_hits = (atom_type[..., None] == jnp.arange(type_radius.shape[0], dtype=jnp.int32)).astype(jnp.float32)
    radius = lax.optimization_barrier(jnp.sum(type_hits * type_radius, axis=-1))
    inner_radius = radius - radius_offset
    scaled = lax.optimization_barrier(jnp.sum(type_hits * type_scale, axis=-1)) * inner_radius
    return (radius, inner_radius, scaled)

def hct_integral(distance, inner_radius, scaled):
    outer_edge = distance + scaled
    inner_edge = jnp.maximum(inner_radius, jnp.abs(distance - scaled))
    inv_outer = 1.0 / outer_edge
    inv_inner = 1.0 / inner_edge
    gap_sq = inv_outer * inv_outer - inv_inner * inv_inner
    integral = inv_inner - inv_outer + 0.25 * distance * gap_sq
    integral = integral + (0.5 * jnp.log(inner_edge * inv_outer) - 0.25 * scaled * scaled * gap_sq) / distance
    integral = integral + jnp.where(inner_radius < scaled - distance, 2.0 * (1.0 / inner_radius - inv_inner), 0.0)
    return jnp.where(inner_radius < outer_edge, integral, 0.0)

def separation(pos_home, pos_away, shift):
    moved = pos_away + shift[:, :, None]
    separations = pos_home[:, :, :, None] - moved[:, :, None, :]
    return (separations, lax.optimization_barrier(jnp.sum(separations * separations, axis=0)))

def descreen_tile(home, away, shift, on_diagonal, weights, both_sides):
    separations, dist_sq = separation(home[0], away[0], shift)
    distance = jnp.sqrt(jnp.where(on_diagonal, 1.0, dist_sq))
    first_side = lax.optimization_barrier(jnp.sum(weights * hct_integral(distance, home[1][:, :, None], away[2][:, None, :]), axis=2))
    if both_sides:
        second_side = lax.optimization_barrier(jnp.sum(weights * hct_integral(distance, away[1][:, None, :], home[2][:, :, None]), axis=1))
    else:
        second_side = first_side
    return (first_side, second_side)

def screen_tile(home, away, shift, weights, both_sides):
    separations, dist_sq = separation(home[0], away[0], shift)
    radii_prod = home[1][:, :, None] * away[1][:, None, :]
    damping = jnp.exp(-dist_sq / (4.0 * radii_prod))
    inv_length = 1.0 / jnp.sqrt(dist_sq + radii_prod * damping)
    charge_prod = weights * home[2][:, :, None] * away[2][:, None, :]
    energy = -0.5 * dielectric_factor * charge_prod * inv_length
    strength = charge_prod * inv_length * inv_length * inv_length
    pulling = -dielectric_factor * strength * (1.0 - 0.25 * damping)
    stretch = 0.5 * dielectric_factor * strength * damping * (1.0 + dist_sq / (4.0 * radii_prod))
    push = pulling[None] * separations
    first_side = jnp.concatenate([lax.optimization_barrier(jnp.sum(push, axis=3)), lax.optimization_barrier(jnp.sum(energy, axis=2))[None], lax.optimization_barrier(jnp.sum(stretch * away[1][:, None, :], axis=2))[None]], axis=0)
    if both_sides:
        second_side = jnp.concatenate([-lax.optimization_barrier(jnp.sum(push, axis=2)), lax.optimization_barrier(jnp.sum(energy, axis=1))[None], lax.optimization_barrier(jnp.sum(stretch * home[1][:, :, None], axis=1))[None]], axis=0)
    else:
        second_side = first_side
    return (first_side, second_side)

def reference(offsets, charges, atom_type, type_radius, type_scale, tile_mask):
    radius, inner_radius, scaled = atom_terms(atom_type, type_radius, type_scale)
    positions = jnp.transpose(offsets, (1, 0, 2, 3))
    atoms = charges.shape[-1]

    def rolled(array, step_x, step_y, axes):
        return jnp.roll(array, (-step_x, -step_y), axis=axes)

    def returned(array, step_x, step_y, axes):
        return jnp.roll(array, (step_x, step_y), axis=axes)
    descreen_sum = jnp.zeros(charges.shape, jnp.float32)
    for offset_code in range(12, 25):
        step_x, step_y = (offset_code // 5 - 2, offset_code % 5 - 2)
        on_diagonal = jnp.logical_and(jnp.eye(atoms, dtype=bool), offset_code == 12)[None]
        weights = jnp.where(on_diagonal, 0.0, 1.0)
        shift = jnp.array([[step_x * block_side], [step_y * block_side], [0.0]], dtype=jnp.float32)
        chosen = tile_mask[:, :, offset_code].astype(jnp.float32)[:, :, None]
        home = (positions, inner_radius, scaled)
        away = (rolled(positions, step_x, step_y, (0, 2)), rolled(inner_radius, step_x, step_y, (0, 1)), rolled(scaled, step_x, step_y, (0, 1)))
        first_side, second_side = lax.map(lambda items: descreen_tile(items[0], items[1], shift, on_diagonal, weights, True), (home, away))
        descreen_sum = descreen_sum + chosen * first_side
        if offset_code != 12:
            descreen_sum = descreen_sum + returned(chosen * second_side, step_x, step_y, (0, 1))
    descreen_psi = 0.5 * inner_radius * descreen_sum
    born_radius = 1.0 / (1.0 / inner_radius - jnp.tanh(descreen_psi * (1.0 - 0.8 * descreen_psi + 4.85 * descreen_psi * descreen_psi)) / radius)
    pair_sum = jnp.zeros((charges.shape[0], 5, charges.shape[1], atoms), jnp.float32)
    for offset_code in range(12, 25):
        step_x, step_y = (offset_code // 5 - 2, offset_code % 5 - 2)
        on_diagonal = jnp.logical_and(jnp.eye(atoms, dtype=bool), offset_code == 12)[None]
        weights = jnp.where(on_diagonal, 0.0, 1.0)
        shift = jnp.array([[step_x * block_side], [step_y * block_side], [0.0]], dtype=jnp.float32)
        chosen = tile_mask[:, :, offset_code].astype(jnp.float32)[:, None, :, None]
        home = (positions, born_radius, charges)
        away = (rolled(positions, step_x, step_y, (0, 2)), rolled(born_radius, step_x, step_y, (0, 1)), rolled(charges, step_x, step_y, (0, 1)))
        first_side, second_side = lax.map(lambda items: screen_tile(items[0], items[1], shift, weights, True), (home, away))
        pair_sum = pair_sum + chosen * first_side
        if offset_code != 12:
            pair_sum = pair_sum + returned(chosen * second_side, step_x, step_y, (0, 2))
    charge_sq = charges * charges
    force = jnp.transpose(pair_sum[:, 0:3], (1, 0, 2, 3))
    atom_energy = pair_sum[:, 3] - 0.5 * dielectric_factor * charge_sq / born_radius
    born_grad = pair_sum[:, 4] + 0.5 * dielectric_factor * charge_sq / (born_radius * born_radius)
    return (born_radius, atom_energy, force, born_grad)
```

```python
import functools

import jax
import jax.numpy as jnp
import numpy as np
from jax import lax
from jax.experimental import pallas as pl
from jax.experimental.pallas import tpu as pltpu
from jax.sharding import PartitionSpec as P

dielectric_factor = 1.0 - 1.0 / 78.5
radius_offset = 0.09
block_side = 8.0
log2e = 1.4426950408889634
ln2 = 0.6931471805599453
f32 = jnp.float32
bf16 = jnp.bfloat16

near_steps = ((0, 1), (1, -1), (1, 0), (1, 1))
far_steps = ((0, 2), (1, -2), (1, 2), (2, -2), (2, -1), (2, 0), (2, 1), (2, 2))
all_steps = near_steps + far_steps


def series_coefficients():
    top = (0.85 * 1.91 / 9.0) ** 2 * 1.001
    nodes = 0.5 * top * (1.0 + np.cos(np.pi * (np.arange(4) + 0.5) / 4))
    exact = sum(2.0 * (k + 1) / (2 * k + 3) * nodes**k for k in range(40))
    return [float(c) for c in np.polynomial.polynomial.polyfit(nodes, exact, 3)]


series = series_coefficients()
chunk = 64


def step_tables():
    scale = np.ones((13, 8))
    shift = np.zeros((13, 8))
    scale[12, 5:8] = 0.0
    for k, (ox, oy) in enumerate(all_steps):
        scale[k, 5:8] = (16 * ox, 16 * oy, 64 * (ox * ox + oy * oy))
        shift[k, 0:2] = (8 * ox, 8 * oy)
    none = np.zeros_like(shift)
    scale = np.concatenate([scale] * 6, axis=1)
    shift = np.concatenate([shift, none, shift, none, none, shift], axis=1)
    tables = np.stack([scale, shift])[..., None] * np.ones(128)
    return jnp.asarray(tables, bf16)


def from_behind(value, axis, steps):
    count = lax.axis_size(axis)
    pairs = [(source, (source + steps) % count) for source in range(count)]
    return lax.ppermute(value, axis, pairs)


def padded(array, sides, width):
    for axis, dim in sides:
        count, length = (lax.axis_size(axis), array.shape[dim])
        up = [(i, (i + 1) % count) for i in range(count)]
        down = [(j, i) for i, j in up]
        last = lax.slice_in_dim(array, length - width, length, axis=dim)
        leading = lax.slice_in_dim(array, 0, width, axis=dim)
        before = lax.ppermute(last, axis, up)
        after = lax.ppermute(leading, axis, down)
        array = jnp.concatenate([before, array, after], axis=dim)
    return array


def atom_terms(atom_type, type_radius, type_scale):
    type_hits = (atom_type[..., None] == jnp.arange(type_radius.shape[0], dtype=jnp.int32)).astype(
        jnp.float32
    )
    radius = jnp.sum(type_hits * type_radius, axis=-1)
    inner_radius = radius - radius_offset
    scaled = jnp.sum(type_hits * type_scale, axis=-1) * inner_radius
    return (radius, inner_radius, scaled)


def split3(value):
    first = value.astype(bf16).astype(f32)
    rest = value - first
    second = rest.astype(bf16).astype(f32)
    return first, second, rest - second


def dot(a, b, ca, cb):
    return lax.dot_general(a, b, (((ca,), (cb,)), ((), ())), preferred_element_type=f32)


def sublane(shape=(8, 128)):
    return lax.broadcasted_iota(jnp.int32, shape, 0)


def squared_length(xyz):
    square = xyz * xyz
    return jnp.sum(square, axis=0, keepdims=True)


def centred(raw):
    row = sublane()
    middle = jnp.where(row < 2, 4.0, 8.0)
    return jnp.where(row < 3, raw - middle, 0.0)


def away_operand(xyz):
    length = squared_length(xyz)
    row = sublane()
    value = jnp.where(row < 3, xyz, jnp.where(row == 4, length, 1.0))
    value = jnp.where(row == 5, xyz[0:1], jnp.where(row == 6, xyz[1:2], value))
    step = jnp.where(row == 4, 2.0, 4.0)
    first = jnp.round(value * step) * (1.0 / step)
    rest = value - first
    second = rest.astype(bf16).astype(f32)
    third = rest - second
    return jnp.concatenate([first, second, first, second, third, first], axis=0).astype(bf16)


def home_operand(xyz, factor):
    length = squared_length(xyz)
    row = sublane()
    value = jnp.where(row < 3, -2.0 * xyz, jnp.where(row == 3, length, 1.0)) * factor
    first, second, third = split3(value)
    stacked = jnp.concatenate([first, first, second, second, first, third], axis=0)
    return jnp.transpose(stacked).astype(bf16)


def lanes_of(rows, k):
    return jnp.broadcast_to(rows[:, k : k + 1], (128, 128))


def fold(value):
    return jnp.sum(value.reshape(-1, 8, 128), axis=0)


def row_totals(value, eye):
    return fold(jnp.sum(value, axis=1, keepdims=True) * eye)


def close_integral(distance, inverse, a, s, whole):
    quarter, log_factor = 0.25 * inverse, (0.5 * ln2) * inverse
    outer = distance + s
    span = distance - s
    inner = jnp.maximum(jnp.abs(span) if whole else span, a)
    inner = jnp.minimum(inner, outer)
    inv_outer = 1.0 / outer
    inv_inner = 1.0 / inner
    part = (inv_inner - inv_outer) * (
        1.0 - (outer * span) * quarter * (inv_inner + inv_outer)
    )
    total = part + log_factor * (jnp.log2(inner) - jnp.log2(outer))
    if whole:
        total = total + 2.0 * (1.0 / a - 1.0 / jnp.maximum(a, -span))
    return total


def descreen_kernel(
    dims, mask_ref, flag_ref, raw_ref, table_ref, out_ref, away_ref, near_ref, even_sq, odd_sq, even_cols, odd_cols, acc_ref
):
    rows_x, rows_y = dims
    width = rows_y + 4
    slots = (rows_x + 2) * width
    homes = rows_x * rows_y

    def prepare(slot):
        raw = raw_ref[slot]
        xyz = centred(raw)
        away_ref[slot] = away_operand(xyz)
        out_ref[slot] = jnp.zeros((8, 128), f32)
        s = raw[4:5]
        sq = s * s
        cube = s * sq
        near_ref[slot] = jnp.concatenate(
            [raw[3:5], series[0] * cube, series[1] * cube * sq, series[2] * cube * (sq * sq), series[3] * cube * (sq * sq) * sq, jnp.zeros((2, 128), f32)], axis=0
        )

    def prepare_turn(n, carry):
        for k in range(4):
            prepare(4 * n + k)
        return carry

    lax.fori_loop(0, slots // 4, prepare_turn, 0)
    eye = (
        lax.broadcasted_iota(jnp.int32, (128, 128), 0)
        == lax.broadcasted_iota(jnp.int32, (128, 128), 1)
    ).astype(f32)

    def slot_of(n):
        block_x = n // rows_y
        return block_x * width + 2 + (n - block_x * rows_y)

    def distances(n, sq_ref, cols_ref):
        slot = slot_of(n)
        left = home_operand(centred(raw_ref[slot]), 1.0)
        sq_ref[:, 12 * 128 : 13 * 128] = dot(left, away_ref[slot] * table_ref[0, 12], 1, 0)
        for k0 in range(0, 12, 2):
            right = []
            for k in (k0, k0 + 1):
                there = slot + all_steps[k][0] * width + all_steps[k][1]
                right.append(away_ref[there] * table_ref[0, k] + table_ref[1, k])
            sq_ref[:, 128 * k0 : 128 * k0 + 256] = dot(left, jnp.concatenate(right, axis=1), 1, 0)
        columns = jnp.transpose(near_ref[slot])
        for k in range(6):
            cols_ref[k] = lanes_of(columns, k)

    def pairs(n, sq_ref, cols_ref, whole):
        slot = slot_of(n)
        here = near_ref[slot]
        for c in range(0, 128, chunk):
            part = pl.ds(c, chunk)
            own = sq_ref[part, 12 * 128 : 13 * 128] + eye[c : c + chunk]
            inverse = lax.rsqrt(own)
            total = close_integral(own * inverse, inverse, cols_ref[0, part], here[1:2], whole)
            acc_ref[part] = total * (1.0 - eye[c : c + chunk])
        for k in range(12):
            there = slot + all_steps[k][0] * width + all_steps[k][1]
            ox, oy = all_steps[k]
            m = mask_ref[n * 25 + (ox + 2) * 5 + oy + 2].astype(f32)
            near = near_ref[there]
            backs = 0.0
            for c in range(0, 128, chunk):
                part = pl.ds(c, chunk)
                sq = sq_ref[part, 128 * k : 128 * k + 128]
                if k < 4:
                    inverse = lax.rsqrt(sq)
                    distance = sq * inverse
                    total = close_integral(distance, inverse, cols_ref[0, part], near[1:2] * m, whole)
                    back = close_integral(distance, inverse, near[0:1] + (1.0 - m) * 1e9, cols_ref[1, part], whole)
                else:
                    rows = near * m
                    w = 1.0 / sq
                    ww = w * w
                    total = ww * (rows[2:3] + w * (rows[3:4] + w * (rows[4:5] + w * rows[5:6])))
                    back = ww * (cols_ref[2, part] + w * (cols_ref[3, part] + w * (cols_ref[4, part] + w * cols_ref[5, part])))
                acc_ref[part] += total
                backs = backs + fold(back)
            out_ref[there] += backs if k < 4 else m * backs
        out_ref[slot] += row_totals(acc_ref[...], eye)

    def turns(whole):
        distances(0, even_sq, even_cols)

        def turn(i, carry):
            n = 2 * i
            distances(n + 1, odd_sq, odd_cols)
            pairs(n, even_sq, even_cols, whole)
            distances(jnp.minimum(n + 2, homes - 1), even_sq, even_cols)
            pairs(n + 1, odd_sq, odd_cols, whole)
            return carry

        lax.fori_loop(0, homes // 2, turn, 0)

    @pl.when(flag_ref[0] == 0)
    def _():
        turns(False)

    @pl.when(flag_ref[0] != 0)
    def _():
        turns(True)


def screen_kernel(
    dims, mask_ref, raw_ref, born_ref, table_ref, away_ref, moment_ref, out_ref, rows_ref, vec_ref,
    even_sq, odd_sq, even_cols, odd_cols, even_high, odd_high, even_low, odd_low, acc_ref,
):
    rows_x, rows_y = dims
    width = rows_y + 4
    slots = (rows_x + 2) * width
    homes = rows_x * rows_y

    def prepare(slot):
        raw = raw_ref[slot]
        xyz = centred(raw)
        born = born_ref[pl.ds(slot, 1), :]
        inv = 1.0 / born
        half = lax.rsqrt(born)
        charge = raw[5:6]
        weak = charge * half
        strong = weak * inv
        block_x = slot // width
        block_y = slot - block_x * width
        x = xyz[0:1] + 8.0 * (block_x.astype(f32) - 0.5 * (rows_x + 1))
        y = xyz[1:2] + 8.0 * (block_y.astype(f32) - 0.5 * (width - 1))
        vector = jnp.concatenate([strong, strong * x, strong * y, strong * xyz[2:3]], axis=0)
        first, second, third = split3(vector)
        vec_ref[slot] = jnp.concatenate([first, second, third, jnp.zeros((4, 128), f32)], axis=0).astype(bf16)
        rows_ref[slot] = jnp.concatenate([inv, -log2e * inv, weak, jnp.zeros((5, 128), f32)], axis=0)
        out_ref[slot] = jnp.zeros((16, 128), f32)
        moment_ref[slot] = jnp.zeros((16, 128), f32)

    def prepare_turn(n, carry):
        for k in range(4):
            prepare(4 * n + k)
        return carry

    lax.fori_loop(0, slots // 4, prepare_turn, 0)
    odd_high[...] = jnp.zeros_like(odd_high)
    odd_low[...] = jnp.zeros_like(odd_low)
    eye = (
        lax.broadcasted_iota(jnp.int32, (128, 128), 0)
        == lax.broadcasted_iota(jnp.int32, (128, 128), 1)
    ).astype(f32)

    def pair_terms(scaled_sq, rows):
        t = scaled_sq * rows[0:1]
        e = 0.25 * jnp.exp2(scaled_sq * rows[1:2])
        inv = lax.rsqrt(t + e)
        cube = inv * inv * inv
        damped = e * cube
        return inv, cube - damped, damped + damped * t

    def slot_of(n):
        block_x = n // rows_y
        return block_x * width + 2 + (n - block_x * rows_y)

    def mask_of(n, k):
        ox, oy = all_steps[k]
        return mask_ref[n * 25 + (ox + 2) * 5 + oy + 2].astype(f32)

    def away_of(slot, k):
        return slot + all_steps[k][0] * width + all_steps[k][1]

    def distances(n, sq_ref, cols_ref):
        slot = slot_of(n)
        here = rows_ref[slot]
        left = home_operand(centred(raw_ref[slot]), 0.25 * here[0:1])
        cols_ref[...] = lanes_of(jnp.transpose(here), 2)
        sq_ref[:, 12 * 128 : 13 * 128] = dot(left, away_ref[slot] * table_ref[0, 12], 1, 0)
        for k0 in range(0, 12, 2):
            right = [away_ref[away_of(slot, k)] * table_ref[0, k] + table_ref[1, k] for k in (k0, k0 + 1)]
            sq_ref[:, 128 * k0 : 128 * k0 + 256] = dot(left, jnp.concatenate(right, axis=1), 1, 0)

    def pairs(n, sq_ref, cols_ref, high_ref, low_ref):
        slot = slot_of(n)
        here = rows_ref[slot]

        def keep(part, k, pull):
            high = pull.astype(bf16)
            high_ref[part, 128 * k : 128 * k + 128] = high
            low_ref[part, 128 * k : 128 * k + 128] = (pull - high.astype(f32)).astype(bf16)

        for c in range(0, 128, chunk):
            part = pl.ds(c, chunk)
            inv, pull, stretch = pair_terms(sq_ref[part, 12 * 128 : 13 * 128], here)
            off = 1.0 - eye[c : c + chunk]
            weak = off * here[2:3]
            acc_ref[0, part] = inv * weak
            acc_ref[1, part] = stretch * weak
            keep(part, 12, pull * off)
        for k in range(12):
            there = away_of(slot, k)
            rows = rows_ref[there]
            m = mask_of(n, k)
            weak = rows[2:3] * m
            near, far = 0.0, 0.0
            for c in range(0, 128, chunk):
                part = pl.ds(c, chunk)
                inv, pull, stretch = pair_terms(sq_ref[part, 128 * k : 128 * k + 128], rows)
                acc_ref[0, part] += inv * weak
                acc_ref[1, part] += stretch * weak
                near = near + fold(inv * cols_ref[part])
                far = far + fold(stretch * cols_ref[part])
                keep(part, k, pull)
            out_ref[there, 0:8] += m * near
            out_ref[there, 8:16] += m * far
        out_ref[slot, 0:8] += row_totals(acc_ref[0], eye)
        out_ref[slot, 8:16] += row_totals(acc_ref[1], eye)

    def moments(n, high_ref, low_ref):
        slot = slot_of(n)
        own = vec_ref[slot]
        own = jnp.concatenate([own, own], axis=1)
        vectors = [vec_ref[away_of(slot, k)] * mask_of(n, k).astype(bf16) for k in range(12)] + [vec_ref[slot]]
        totals = dot(high_ref[...], jnp.concatenate(vectors, axis=1), 1, 1)
        totals = totals + dot(low_ref[...], jnp.concatenate(vectors, axis=1), 1, 1)
        for k0 in range(0, 12, 2):
            lanes = slice(128 * k0, 128 * k0 + 256)
            back = dot(own, jnp.concatenate([high_ref[:, lanes], low_ref[:, lanes]], axis=0), 1, 0)
            for t in range(2):
                moment_ref[away_of(slot, k0 + t)] += mask_of(n, k0 + t) * back[:, 128 * t : 128 * t + 128]
        moment_ref[slot] += jnp.transpose(totals)

    distances(0, even_sq, even_cols)

    def turn(i, carry):
        n = 2 * i
        distances(n + 1, odd_sq, odd_cols)
        moments(jnp.maximum(n - 1, 0), odd_high, odd_low)
        pairs(n, even_sq, even_cols, even_high, even_low)
        distances(jnp.minimum(n + 2, homes - 1), even_sq, even_cols)
        moments(n, even_high, even_low)
        pairs(n + 1, odd_sq, odd_cols, odd_high, odd_low)
        return carry

    lax.fori_loop(0, homes // 2, turn, 0)
    moments(homes - 1, odd_high, odd_low)


def descreen(dims, mask, flag, raw, table):
    slots = raw.shape[0]
    smem = pl.BlockSpec(memory_space=pltpu.SMEM)
    vmem = pl.BlockSpec(memory_space=pltpu.VMEM)
    return pl.pallas_call(
        functools.partial(descreen_kernel, dims),
        out_shape=(
            jax.ShapeDtypeStruct((slots, 8, 128), f32),
            jax.ShapeDtypeStruct((slots, 48, 128), bf16),
        ),
        in_specs=[smem, smem, vmem, vmem],
        out_specs=(vmem, vmem),
        scratch_shapes=[
            pltpu.VMEM((slots, 8, 128), f32),
            pltpu.VMEM((128, 13 * 128), f32),
            pltpu.VMEM((128, 13 * 128), f32),
            pltpu.VMEM((6, 128, 128), f32),
            pltpu.VMEM((6, 128, 128), f32),
            pltpu.VMEM((128, 128), f32),
        ],
        compiler_params=pltpu.CompilerParams(vmem_limit_bytes=56 * 2**20),
        name="descreen",
    )(mask, flag, raw, table)


def screen(dims, mask, raw, born, table, away):
    slots = raw.shape[0]
    smem = pl.BlockSpec(memory_space=pltpu.SMEM)
    vmem = pl.BlockSpec(memory_space=pltpu.VMEM)
    return pl.pallas_call(
        functools.partial(screen_kernel, dims),
        out_shape=(
            jax.ShapeDtypeStruct((slots, 16, 128), f32),
            jax.ShapeDtypeStruct((slots, 16, 128), f32),
        ),
        in_specs=[smem, vmem, vmem, vmem, vmem],
        out_specs=(vmem, vmem),
        scratch_shapes=[
            pltpu.VMEM((slots, 8, 128), f32),
            pltpu.VMEM((slots, 16, 128), bf16),
            pltpu.VMEM((128, 13 * 128), f32),
            pltpu.VMEM((128, 13 * 128), f32),
            pltpu.VMEM((128, 128), f32),
            pltpu.VMEM((128, 128), f32),
            pltpu.VMEM((128, 13 * 128), bf16),
            pltpu.VMEM((128, 13 * 128), bf16),
            pltpu.VMEM((128, 13 * 128), bf16),
            pltpu.VMEM((128, 13 * 128), bf16),
            pltpu.VMEM((2, 128, 128), f32),
        ],
        compiler_params=pltpu.CompilerParams(vmem_limit_bytes=56 * 2**20),
        name="screen",
    )(mask, raw, born, table, away)


def fold_columns(columns, rows_y):
    folded = columns[:, :, 4 : rows_y + 4]
    folded = folded.at[:, :, 0:2].add(columns[:, :, 0:2])
    folded = folded.at[:, :, rows_y - 2 : rows_y].add(columns[:, :, rows_y + 6 : rows_y + 8])
    return folded


def settle(extended, rows_x, rows_y):
    arriving = from_behind(extended[:, rows_x : rows_x + 2], "gx", 1)
    middle = extended[:, 0:rows_x].at[:, 0:2].add(arriving)
    columns = padded(middle, (("gy", 2),), 2)
    return fold_columns(columns, rows_y)


def body(offsets, charges, atom_type, type_radius, type_scale, tile_mask):
    rows_x, rows_y, atoms = charges.shape
    width = rows_y + 4
    slots = (rows_x + 2) * width
    radius, inner_radius, scaled = atom_terms(atom_type, type_radius, type_scale)
    zero = jnp.zeros_like(charges)
    payload = jnp.stack([offsets[0], offsets[1], offsets[2], inner_radius, scaled, charges], axis=2)
    widened = padded(payload, (("gy", 1),), 2)
    ahead = from_behind(widened[0:2], "gx", -1)
    raw = jnp.concatenate([widened, ahead], axis=0).reshape(slots, 6, atoms)
    raw = jnp.concatenate([raw, jnp.zeros((slots, 2, atoms), f32)], axis=1)
    mask = tile_mask.reshape(-1)
    type_inner = type_radius - radius_offset
    flag = (jnp.max(type_scale * type_inner) - 0.99 > jnp.min(type_inner)).astype(jnp.int32)[None]
    table = step_tables()
    dims = (rows_x, rows_y)
    sums, away = descreen(dims, mask, flag, raw, table)
    sums = jnp.sum(sums, axis=1).reshape(1, rows_x + 2, width, atoms)
    descreen_sum = settle(sums, rows_x, rows_y)[0]
    descreen_psi = 0.5 * inner_radius * descreen_sum
    born_radius = 1.0 / (
        1.0 / inner_radius
        - jnp.tanh(descreen_psi * (1.0 - 0.8 * descreen_psi + 4.85 * descreen_psi * descreen_psi))
        / radius
    )
    born_wide = padded(born_radius, (("gy", 1),), 2)
    born_next = from_behind(born_wide[0:2], "gx", -1)
    born_ext = jnp.concatenate([born_wide, born_next], axis=0).reshape(slots, atoms)

    raw_moments, raw_sums = screen(dims, mask, raw, born_ext, table, away)
    half = lax.rsqrt(born_ext)
    weak = raw[:, 5] * half
    strong = weak / born_ext
    slot = jnp.arange(slots, dtype=jnp.int32)[:, None]
    x = raw[:, 0] - 4.0 + 8.0 * ((slot // width).astype(f32) - 0.5 * (rows_x + 1))
    y = raw[:, 1] - 4.0 + 8.0 * ((slot % width).astype(f32) - 0.5 * (width - 1))
    z = raw[:, 2] - 8.0
    moments = [raw_moments[:, k] + raw_moments[:, 4 + k] + raw_moments[:, 8 + k] for k in range(4)]
    scale = (-dielectric_factor / 8.0) * strong
    pair_sum = jnp.stack(
        [
            scale * (x * moments[0] - moments[1]),
            scale * (y * moments[0] - moments[2]),
            scale * (z * moments[0] - moments[3]),
            (-0.25 * dielectric_factor) * weak * jnp.sum(raw_sums[:, 0:8], axis=1),
            (0.25 * dielectric_factor) * strong * jnp.sum(raw_sums[:, 8:16], axis=1),
        ],
        axis=0,
    ).reshape(5, rows_x + 2, width, atoms)
    pair_sum = settle(pair_sum, rows_x, rows_y)
    charge_sq = charges * charges
    force = pair_sum[0:3]
    atom_energy = pair_sum[3] - 0.5 * dielectric_factor * charge_sq / born_radius
    born_grad = pair_sum[4] + 0.5 * dielectric_factor * charge_sq / (born_radius * born_radius)
    return (born_radius, atom_energy, force, born_grad)


def solution(mesh):
    placed = (
        P(None, "gx", "gy", None),
        P("gx", "gy", None),
        P("gx", "gy", None),
        P(),
        P(),
        P("gx", "gy", None),
    )
    return jax.shard_map(
        body,
        mesh=mesh,
        in_specs=placed,
        out_specs=(
            P("gx", "gy", None),
            P("gx", "gy", None),
            P(None, "gx", "gy", None),
            P("gx", "gy", None),
        ),
        check_vma=False,
    )
```

```python
import functools

import jax
import jax.numpy as jnp
import numpy as np
from jax import lax
from jax.experimental import pallas as pl
from jax.experimental.pallas import tpu as pltpu
from jax.sharding import PartitionSpec as P

dielectric_factor = 1.0 - 1.0 / 78.5
radius_offset = 0.09
block_side = 8.0
log2e = 1.4426950408889634
ln2 = 0.6931471805599453
f32 = jnp.float32
bf16 = jnp.bfloat16

near_steps = ((0, 1), (1, -1), (1, 0), (1, 1))
far_steps = ((0, 2), (1, -2), (1, 2), (2, -2), (2, -1), (2, 0), (2, 1), (2, 2))
all_steps = near_steps + far_steps


def series_coefficients():
    top = (0.85 * 1.91 / 9.0) ** 2 * 1.001
    nodes = 0.5 * top * (1.0 + np.cos(np.pi * (np.arange(4) + 0.5) / 4))
    exact = sum(2.0 * (k + 1) / (2 * k + 3) * nodes**k for k in range(40))
    return [float(c) for c in np.polynomial.polynomial.polyfit(nodes, exact, 3)]


series = series_coefficients()
chunk = 64


def step_tables():
    scale = np.ones((13, 8))
    shift = np.zeros((13, 8))
    scale[12, 5:8] = 0.0
    for k, (ox, oy) in enumerate(all_steps):
        scale[k, 5:8] = (16 * ox, 16 * oy, 64 * (ox * ox + oy * oy))
        shift[k, 0:2] = (8 * ox, 8 * oy)
    none = np.zeros_like(shift)
    scale = np.concatenate([scale] * 6, axis=1)
    shift = np.concatenate([shift, none, shift, none, none, shift], axis=1)
    tables = np.stack([scale, shift])[..., None] * np.ones(128)
    return jnp.asarray(tables, bf16)


def split3(value):
    first = value.astype(bf16).astype(f32)
    rest = value - first
    second = rest.astype(bf16).astype(f32)
    return first, second, rest - second


def dot(a, b, ca, cb):
    return lax.dot_general(a, b, (((ca,), (cb,)), ((), ())), preferred_element_type=f32)


def sublane(shape=(8, 128)):
    return lax.broadcasted_iota(jnp.int32, shape, 0)


def squared_length(xyz):
    square = xyz * xyz
    return jnp.sum(square, axis=0, keepdims=True)


def centred(raw):
    row = sublane()
    middle = jnp.where(row < 2, 4.0, 8.0)
    return jnp.where(row < 3, raw - middle, 0.0)


def away_operand(xyz):
    length = squared_length(xyz)
    row = sublane()
    value = jnp.where(row < 3, xyz, jnp.where(row == 4, length, 1.0))
    value = jnp.where(row == 5, xyz[0:1], jnp.where(row == 6, xyz[1:2], value))
    step = jnp.where(row == 4, 2.0, 4.0)
    first = jnp.round(value * step) * (1.0 / step)
    rest = value - first
    second = rest.astype(bf16).astype(f32)
    third = rest - second
    return jnp.concatenate([first, second, first, second, third, first], axis=0).astype(bf16)


def home_operand(xyz, factor):
    length = squared_length(xyz)
    row = sublane()
    value = jnp.where(row < 3, -2.0 * xyz, jnp.where(row == 3, length, 1.0)) * factor
    first, second, third = split3(value)
    stacked = jnp.concatenate([first, first, second, second, first, third], axis=0)
    return jnp.transpose(stacked).astype(bf16)


def lanes_of(rows, k):
    return jnp.broadcast_to(rows[:, k : k + 1], (128, 128))


def fold(value):
    return jnp.sum(value.reshape(-1, 8, 128), axis=0)


def row_totals(value, eye):
    return fold(jnp.sum(value, axis=1, keepdims=True) * eye)


def close_integral(distance, quarter, log_factor, a, s, whole):
    outer = distance + s
    span = distance - s
    inner = jnp.maximum(jnp.abs(span) if whole else span, a)
    inner = jnp.minimum(inner, outer)
    inv_outer = 1.0 / outer
    inv_inner = 1.0 / inner
    ratio = outer * inv_inner
    total = (inv_inner - inv_outer) * (1.0 - (span * quarter) * (ratio + 1.0))
    total = total + log_factor * jnp.log2(ratio)
    if whole:
        total = total + 2.0 * (1.0 / a - 1.0 / jnp.maximum(a, -span))
    return total


def weave(*parts):
    live = list(parts)
    while live:
        for part in list(live):
            for _ in range(2 if part is parts[-1] and len(parts) > 1 else 1):
                if next(part, live) is live:
                    live.remove(part)
                    break


def descreen_kernel(
    dims, mask_ref, flag_ref, raw_ref, table_ref, out_ref, away_ref, near_ref, even_sq, odd_sq, even_cols, odd_cols, acc_ref
):
    rows_x, rows_y = dims
    width = rows_y + 4
    slots = (rows_x + 2) * width
    homes = rows_x * rows_y

    def prepare(slot):
        raw = raw_ref[slot]
        xyz = centred(raw)
        away_ref[slot] = away_operand(xyz)
        out_ref[slot] = jnp.zeros((8, 128), f32)
        s = raw[4:5]
        sq = s * s
        cube = s * sq
        near_ref[slot] = jnp.concatenate(
            [raw[3:5], series[0] * cube, series[1] * cube * sq, series[2] * cube * (sq * sq), series[3] * cube * (sq * sq) * sq, jnp.zeros((2, 128), f32)], axis=0
        )

    def prepare_turn(n, carry):
        for k in range(4):
            prepare(4 * n + k)
        return carry

    lax.fori_loop(0, slots // 4, prepare_turn, 0)
    eye = (
        lax.broadcasted_iota(jnp.int32, (128, 128), 0)
        == lax.broadcasted_iota(jnp.int32, (128, 128), 1)
    ).astype(f32)

    def slot_of(n):
        block_x = n // rows_y
        return block_x * width + 2 + (n - block_x * rows_y)

    def distances(n, sq_ref, cols_ref):
        slot = slot_of(n)
        left = home_operand(centred(raw_ref[slot]), 1.0)
        columns = jnp.transpose(near_ref[slot])
        sq_ref[:, 12 * 128 : 13 * 128] = dot(left, away_ref[slot] * table_ref[0, 12], 1, 0)
        cols_ref[0] = lanes_of(columns, 0)
        yield
        for k0 in range(0, 12, 2):
            right = []
            for k in (k0, k0 + 1):
                there = slot + all_steps[k][0] * width + all_steps[k][1]
                right.append(away_ref[there] * table_ref[0, k] + table_ref[1, k])
            sq_ref[:, 128 * k0 : 128 * k0 + 256] = dot(left, jnp.concatenate(right, axis=1), 1, 0)
            if k0 < 10:
                cols_ref[k0 // 2 + 1] = lanes_of(columns, k0 // 2 + 1)
            yield

    def pairs(n, sq_ref, cols_ref, whole):
        slot = slot_of(n)
        here = near_ref[slot]
        for c in range(0, 128, chunk):
            part = pl.ds(c, chunk)
            own = sq_ref[part, 12 * 128 : 13 * 128] + eye[c : c + chunk]
            inverse = lax.rsqrt(own)
            total = close_integral(own * inverse, 0.25 * inverse, (-0.5 * ln2) * inverse, cols_ref[0, part], here[1:2], whole)
            acc_ref[part] = total * (1.0 - eye[c : c + chunk])
        yield
        for k in range(12):
            there = slot + all_steps[k][0] * width + all_steps[k][1]
            ox, oy = all_steps[k]
            m = mask_ref[n * 25 + (ox + 2) * 5 + oy + 2].astype(f32)
            near = near_ref[there]
            backs = 0.0
            for c in range(0, 128, chunk):
                part = pl.ds(c, chunk)
                sq = sq_ref[part, 128 * k : 128 * k + 128]
                if k < 4:
                    inverse = lax.rsqrt(sq)
                    distance = sq * inverse
                    scales = (0.25 * inverse, (-0.5 * ln2) * inverse)
                    total = close_integral(distance, *scales, cols_ref[0, part], near[1:2] * m, whole)
                    back = close_integral(distance, *scales, near[0:1] + (1.0 - m) * 1e9, cols_ref[1, part], whole)
                else:
                    rows = near * m
                    w = 1.0 / sq
                    ww = w * w
                    total = ww * (rows[2:3] + w * (rows[3:4] + w * (rows[4:5] + w * rows[5:6])))
                    back = ww * (cols_ref[2, part] + w * (cols_ref[3, part] + w * (cols_ref[4, part] + w * cols_ref[5, part])))
                acc_ref[part] += total
                backs = backs + fold(back)
            out_ref[there] += backs if k < 4 else m * backs
            yield
        out_ref[slot] += row_totals(acc_ref[...], eye)
        yield

    def turns(whole):
        weave(distances(0, even_sq, even_cols))

        def turn(i, carry):
            n = 2 * i
            weave(distances(n + 1, odd_sq, odd_cols), pairs(n, even_sq, even_cols, whole))
            weave(
                distances(jnp.minimum(n + 2, homes - 1), even_sq, even_cols),
                pairs(n + 1, odd_sq, odd_cols, whole),
            )
            return carry

        lax.fori_loop(0, homes // 2, turn, 0)

    @pl.when(flag_ref[0] == 0)
    def _():
        turns(False)

    @pl.when(flag_ref[0] != 0)
    def _():
        turns(True)


def screen_kernel(
    dims, mask_ref, raw_ref, born_ref, table_ref, away_ref, moment_ref, out_ref, rows_ref, vec_ref,
    even_sq, odd_sq, even_cols, odd_cols, even_high, odd_high, even_low, odd_low, acc_ref,
):
    rows_x, rows_y = dims
    width = rows_y + 4
    slots = (rows_x + 2) * width
    homes = rows_x * rows_y

    def prepare(slot):
        raw = raw_ref[slot]
        xyz = centred(raw)
        born = born_ref[slot]
        inv = 1.0 / born
        half = lax.rsqrt(born)
        charge = raw[5:6]
        weak = charge * half
        strong = weak * inv
        block_x = slot // width
        block_y = slot - block_x * width
        x = xyz[0:1] + 8.0 * (block_x.astype(f32) - 0.5 * (rows_x + 1))
        y = xyz[1:2] + 8.0 * (block_y.astype(f32) - 0.5 * (width - 1))
        vector = jnp.concatenate([strong, strong * x, strong * y, strong * xyz[2:3]], axis=0)
        first, second, third = split3(vector)
        vec_ref[slot] = jnp.concatenate([first, second, third, jnp.zeros((4, 128), f32)], axis=0).astype(bf16)
        rows_ref[slot] = jnp.concatenate([inv, -log2e * inv, weak, jnp.zeros((5, 128), f32)], axis=0)
        out_ref[slot] = jnp.zeros((16, 128), f32)
        moment_ref[slot] = jnp.zeros((16, 128), f32)

    def prepare_turn(n, carry):
        for k in range(4):
            prepare(4 * n + k)
        return carry

    lax.fori_loop(0, slots // 4, prepare_turn, 0)
    odd_high[...] = jnp.zeros_like(odd_high)
    odd_low[...] = jnp.zeros_like(odd_low)
    eye = (
        lax.broadcasted_iota(jnp.int32, (128, 128), 0)
        == lax.broadcasted_iota(jnp.int32, (128, 128), 1)
    ).astype(f32)

    def pair_terms(scaled_sq, rows):
        t = scaled_sq * rows[0:1]
        e = 0.25 * jnp.exp2(scaled_sq * rows[1:2])
        inv = lax.rsqrt(t + e)
        cube = inv * inv * inv
        damped = e * cube
        return inv, cube - damped, damped + damped * t

    def slot_of(n):
        block_x = n // rows_y
        return block_x * width + 2 + (n - block_x * rows_y)

    def mask_of(n, k):
        ox, oy = all_steps[k]
        return mask_ref[n * 25 + (ox + 2) * 5 + oy + 2].astype(f32)

    def away_of(slot, k):
        return slot + all_steps[k][0] * width + all_steps[k][1]

    def distances(n, sq_ref, cols_ref):
        slot = slot_of(n)
        here = rows_ref[slot]
        left = home_operand(centred(raw_ref[slot]), 0.25 * here[0:1])
        cols_ref[...] = lanes_of(jnp.transpose(here), 2)
        sq_ref[:, 12 * 128 : 13 * 128] = dot(left, away_ref[slot] * table_ref[0, 12], 1, 0)
        yield
        for k0 in range(0, 12, 2):
            right = [away_ref[away_of(slot, k)] * table_ref[0, k] + table_ref[1, k] for k in (k0, k0 + 1)]
            sq_ref[:, 128 * k0 : 128 * k0 + 256] = dot(left, jnp.concatenate(right, axis=1), 1, 0)
            yield

    def pairs(n, sq_ref, cols_ref, high_ref, low_ref):
        slot = slot_of(n)
        here = rows_ref[slot]

        def keep(part, k, pull):
            high = pull.astype(bf16)
            high_ref[part, 128 * k : 128 * k + 128] = high
            low_ref[part, 128 * k : 128 * k + 128] = (pull - high.astype(f32)).astype(bf16)

        for c in range(0, 128, chunk):
            part = pl.ds(c, chunk)
            inv, pull, stretch = pair_terms(sq_ref[part, 12 * 128 : 13 * 128], here)
            off = 1.0 - eye[c : c + chunk]
            weak = off * here[2:3]
            acc_ref[0, part] = inv * weak
            acc_ref[1, part] = stretch * weak
            keep(part, 12, pull * off)
        yield
        for k in range(12):
            there = away_of(slot, k)
            rows = rows_ref[there]
            m = mask_of(n, k)
            weak = rows[2:3] * m
            near, far = 0.0, 0.0
            for c in range(0, 128, chunk):
                part = pl.ds(c, chunk)
                inv, pull, stretch = pair_terms(sq_ref[part, 128 * k : 128 * k + 128], rows)
                acc_ref[0, part] += inv * weak
                acc_ref[1, part] += stretch * weak
                near = near + fold(inv * cols_ref[part])
                far = far + fold(stretch * cols_ref[part])
                keep(part, k, pull)
            out_ref[there, 0:8] += m * near
            out_ref[there, 8:16] += m * far
            yield
        out_ref[slot, 0:8] += row_totals(acc_ref[0], eye)
        out_ref[slot, 8:16] += row_totals(acc_ref[1], eye)
        yield

    def moments(n, high_ref, low_ref):
        slot = slot_of(n)
        own = vec_ref[slot]
        own = jnp.concatenate([own, own], axis=1)
        vectors = [vec_ref[away_of(slot, k)] * mask_of(n, k).astype(bf16) for k in range(12)] + [vec_ref[slot]]
        totals = 0.0
        for k0 in range(0, 12, 2):
            lanes = slice(128 * k0, 128 * k0 + 256)
            back = dot(own, jnp.concatenate([high_ref[:, lanes], low_ref[:, lanes]], axis=0), 1, 0)
            for t in range(2):
                moment_ref[away_of(slot, k0 + t)] += mask_of(n, k0 + t) * back[:, 128 * t : 128 * t + 128]
            if k0 % 4 == 2:
                group = slice(k0 - 2, k0 + 3 if k0 == 10 else k0 + 2)
                lanes = slice(128 * group.start, 128 * group.stop)
                totals = totals + dot(
                    jnp.concatenate([high_ref[:, lanes], low_ref[:, lanes]], axis=1),
                    jnp.concatenate(vectors[group] * 2, axis=1), 1, 1,
                )
            yield
        moment_ref[slot] += jnp.transpose(totals)
        yield

    weave(distances(0, even_sq, even_cols))

    def turn(i, carry):
        for n in (4 * i, 4 * i + 2):
            weave(
                distances(n + 1, odd_sq, odd_cols),
                moments(jnp.maximum(n - 1, 0), odd_high, odd_low),
                pairs(n, even_sq, even_cols, even_high, even_low),
            )
            weave(
                distances(jnp.minimum(n + 2, homes - 1), even_sq, even_cols),
                moments(n, even_high, even_low),
                pairs(n + 1, odd_sq, odd_cols, odd_high, odd_low),
            )
        return carry

    lax.fori_loop(0, homes // 4, turn, 0)
    weave(moments(homes - 1, odd_high, odd_low))


def descreen(dims, mask, flag, raw, table):
    slots = raw.shape[0]
    smem = pl.BlockSpec(memory_space=pltpu.SMEM)
    vmem = pl.BlockSpec(memory_space=pltpu.VMEM)
    return pl.pallas_call(
        functools.partial(descreen_kernel, dims),
        out_shape=(
            jax.ShapeDtypeStruct((slots, 8, 128), f32),
            jax.ShapeDtypeStruct((slots, 48, 128), bf16),
        ),
        in_specs=[smem, smem, vmem, vmem],
        out_specs=(vmem, vmem),
        scratch_shapes=[
            pltpu.VMEM((slots, 8, 128), f32),
            pltpu.VMEM((128, 13 * 128), f32),
            pltpu.VMEM((128, 13 * 128), f32),
            pltpu.VMEM((6, 128, 128), f32),
            pltpu.VMEM((6, 128, 128), f32),
            pltpu.VMEM((128, 128), f32),
        ],
        compiler_params=pltpu.CompilerParams(vmem_limit_bytes=56 * 2**20),
        name="descreen",
    )(mask, flag, raw, table)


def screen(dims, mask, raw, born, table, away):
    slots = raw.shape[0]
    smem = pl.BlockSpec(memory_space=pltpu.SMEM)
    vmem = pl.BlockSpec(memory_space=pltpu.VMEM)
    return pl.pallas_call(
        functools.partial(screen_kernel, dims),
        out_shape=(
            jax.ShapeDtypeStruct((slots, 16, 128), f32),
            jax.ShapeDtypeStruct((slots, 16, 128), f32),
        ),
        in_specs=[smem, vmem, vmem, vmem, vmem],
        out_specs=(vmem, vmem),
        scratch_shapes=[
            pltpu.VMEM((slots, 8, 128), f32),
            pltpu.VMEM((slots, 16, 128), bf16),
            pltpu.VMEM((128, 13 * 128), f32),
            pltpu.VMEM((128, 13 * 128), f32),
            pltpu.VMEM((128, 128), f32),
            pltpu.VMEM((128, 128), f32),
            pltpu.VMEM((128, 13 * 128), bf16),
            pltpu.VMEM((128, 13 * 128), bf16),
            pltpu.VMEM((128, 13 * 128), bf16),
            pltpu.VMEM((128, 13 * 128), bf16),
            pltpu.VMEM((2, 128, 128), f32),
        ],
        compiler_params=pltpu.CompilerParams(vmem_limit_bytes=56 * 2**20),
        name="screen",
    )(mask, raw, born, table, away)


def around(dx, dy):
    count_x, count_y = lax.axis_size("gx"), lax.axis_size("gy")
    return (
        lax.rem(lax.axis_index("gx") + (dx + count_x), count_x),
        lax.rem(lax.axis_index("gy") + (dy + count_y), count_y),
    )


def greet():
    barrier = pltpu.get_barrier_semaphore()
    ring = [(dx, dy) for dx in (-1, 0, 1) for dy in (-1, 0, 1) if (dx, dy) != (0, 0)]
    for dx, dy in ring:
        pl.semaphore_signal(barrier, inc=1, device_id=around(dx, dy), device_id_type=pl.DeviceIdType.MESH)
    pl.semaphore_wait(barrier, len(ring))


def send(src, dst, sems, k, to):
    copy = pltpu.make_async_remote_copy(
        src_ref=src,
        dst_ref=dst,
        send_sem=sems.at[0, k],
        recv_sem=sems.at[1, k],
        device_id=around(*to),
        device_id_type=pl.DeviceIdType.MESH,
    )
    copy.start()
    return copy


def fill_halo(ext, sems, rows_x, rows_y):
    own = pl.ds(2, rows_y)
    top, ahead = pl.ds(0, 2), pl.ds(rows_x, 2)
    body_rows = pl.ds(0, rows_x)
    left, first = pl.ds(0, 2), pl.ds(2, 2)
    last, right = pl.ds(rows_y, 2), pl.ds(rows_y + 2, 2)
    plan = [
        (top, own, ahead, own, (-1, 0)),
        (body_rows, last, body_rows, left, (0, 1)),
        (body_rows, first, body_rows, right, (0, -1)),
        (top, last, ahead, left, (-1, 1)),
        (top, first, ahead, right, (-1, -1)),
    ]
    copies = [
        send(ext.at[rs, cs], ext.at[rd, cd], sems, k, to)
        for k, (rs, cs, rd, cd, to) in enumerate(plan)
    ]
    for copy in copies:
        copy.wait()


def give_back(ext, ahead_land, side_land, corner_land, sems, rows_x, rows_y):
    own = pl.ds(2, rows_y)
    ahead, body_rows = pl.ds(rows_x, 2), pl.ds(0, rows_x)
    left, right = pl.ds(0, 2), pl.ds(rows_y + 2, 2)
    copies = [
        send(ext.at[ahead, own], ahead_land, sems, 0, (1, 0)),
        send(ext.at[body_rows, left], side_land.at[0], sems, 1, (0, -1)),
        send(ext.at[body_rows, right], side_land.at[1], sems, 2, (0, 1)),
        send(ext.at[ahead, left], corner_land.at[0], sems, 3, (1, -1)),
        send(ext.at[ahead, right], corner_land.at[1], sems, 4, (1, 1)),
    ]
    for copy in copies:
        copy.wait()
    ext[0:2, 2 : rows_y + 2] += ahead_land[...]
    ext[0:rows_x, rows_y : rows_y + 2] += side_land[0]
    ext[0:rows_x, 2:4] += side_land[1]
    ext[0:2, rows_y : rows_y + 2] += corner_land[0]
    ext[0:2, 2:4] += corner_land[1]


def gather_kernel(radius_ref, scale_ref, offsets_ref, charge_ref, type_ref, ext, sems):
    rows_x, rows_y, _ = charge_ref.shape
    greet()
    for x in range(rows_x):
        for y in range(0, rows_y, 8):
            types = type_ref[x, y : y + 8]
            radius = jnp.zeros((8, 128), f32)
            scale = jnp.zeros((8, 128), f32)
            for k in range(radius_ref.shape[0]):
                radius = jnp.where(types == k, radius_ref[k], radius)
                scale = jnp.where(types == k, scale_ref[k], scale)
            inner = radius - radius_offset
            parts = [offsets_ref[k, x, y : y + 8] for k in range(3)]
            parts += [inner, scale * inner, charge_ref[x, y : y + 8], radius, jnp.zeros((8, 128), f32)]
            for k, part in enumerate(parts):
                ext[x, 2 + y : 10 + y, k, :] = part
    fill_halo(ext, sems, rows_x, rows_y)


def born_kernel(sum_ref, raw_ref, born_ref, ext, ahead_land, side_land, corner_land, sems):
    width = sum_ref.shape[1]
    rows_x, rows_y = sum_ref.shape[0] - 2, width - 4
    greet()

    def reduce_turn(x, carry):
        for y in range(width):
            ext[x, y] = jnp.sum(sum_ref[x, y], axis=0, keepdims=True)
        return carry

    lax.fori_loop(0, rows_x + 2, reduce_turn, 0)
    give_back(ext, ahead_land, side_land, corner_land, sems.at[0], rows_x, rows_y)

    def radius_turn(x, carry):
        for y in range(2, rows_y + 2):
            raw = raw_ref[x, y]
            inner, radius = raw[3:4], raw[6:7]
            psi = 0.5 * inner * ext[x, y]
            bent = jnp.tanh(psi * (1.0 - 0.8 * psi + 4.85 * psi * psi))
            born_ref[x, y] = 1.0 / (1.0 / inner - bent / radius)
        return carry

    lax.fori_loop(0, rows_x, radius_turn, 0)
    fill_halo(born_ref, sems.at[1], rows_x, rows_y)


def settle_kernel(
    moment_ref, sum_ref, raw_ref, born_ref, born_out, energy_out, force_out, grad_out,
    ext, ahead_land, side_land, corner_land, sems,
):
    width = sum_ref.shape[1]
    rows_x, rows_y = sum_ref.shape[0] - 2, width - 4
    greet()
    row = sublane()

    def finish_turn(x, carry):
        for y in range(width):
            raw = raw_ref[x, y]
            born = born_ref[x, y]
            inv = 1.0 / born
            weak = raw[5:6] * lax.rsqrt(born)
            strong = weak * inv
            moment = moment_ref[x, y]
            moment = moment[0:8] + moment[8:16]
            moment = moment[0:4] + moment[4:8]
            middle = jnp.where(row == 0, 8.0 * (x.astype(f32) - 0.5 * (rows_x + 1)) - 4.0, 8.0 * (y - 0.5 * (width - 1)) - 4.0)
            place = raw + jnp.where(row == 2, -8.0, middle)
            force = ((-dielectric_factor / 8.0) * strong) * (place[0:3] * moment[0:1] - moment[1:4])
            sums = sum_ref[x, y]
            energy = ((-0.25 * dielectric_factor) * weak) * jnp.sum(sums[0:8], axis=0, keepdims=True)
            grad = ((0.25 * dielectric_factor) * strong) * jnp.sum(sums[8:16], axis=0, keepdims=True)
            ext[x, y] = jnp.concatenate([force, energy, grad, jnp.zeros((3, 128), f32)], axis=0)
        return carry

    lax.fori_loop(0, rows_x + 2, finish_turn, 0)
    give_back(ext, ahead_land, side_land, corner_land, sems, rows_x, rows_y)
    for x in range(rows_x):
        for y in range(0, rows_y, 8):
            here = slice(2 + y, 10 + y)
            there = slice(y, y + 8)
            born = born_ref[x, here, 0, :]
            charge = raw_ref[x, here, 5, :]
            own = (0.5 * dielectric_factor) * (charge * charge) / born
            born_out[x, there] = born
            for k in range(3):
                force_out[k, x, there] = ext[x, here, k, :]
            energy_out[x, there] = ext[x, here, 3, :] - own
            grad_out[x, there] = ext[x, here, 4, :] + own / born


def exchange(kernel, ident, ins, outs, scratch):
    smem = pl.BlockSpec(memory_space=pltpu.SMEM)
    vmem = pl.BlockSpec(memory_space=pltpu.VMEM)
    return pl.pallas_call(
        kernel,
        out_shape=tuple(jax.ShapeDtypeStruct(shape, f32) for shape in outs),
        in_specs=[smem if value.ndim == 1 else vmem for value in ins],
        out_specs=tuple(vmem for _ in outs),
        scratch_shapes=scratch,
        compiler_params=pltpu.CompilerParams(
            collective_id=ident, has_side_effects=True, vmem_limit_bytes=56 * 2**20
        ),
        name=kernel.__name__,
    )(*ins)


def landing(rows_x, rows_y, depth):
    return [
        pltpu.VMEM((rows_x + 2, rows_y + 4, depth, 128), f32),
        pltpu.VMEM((2, rows_y, depth, 128), f32),
        pltpu.VMEM((2, rows_x, 2, depth, 128), f32),
        pltpu.VMEM((2, 2, 2, depth, 128), f32),
    ]


def body(offsets, charges, atom_type, type_radius, type_scale, tile_mask):
    rows_x, rows_y, atoms = charges.shape
    dims = (rows_x, rows_y)
    grid = (rows_x + 2, rows_y + 4)
    slots = grid[0] * grid[1]
    dma = pltpu.SemaphoreType.DMA
    (raw,) = exchange(
        gather_kernel, 0, (type_radius, type_scale, offsets, charges, atom_type),
        [grid + (8, atoms)], [dma((2, 5))],
    )
    mask = tile_mask.reshape(-1)
    type_inner = type_radius - radius_offset
    flag = (jnp.max(type_scale * type_inner) - 0.99 > jnp.min(type_inner)).astype(jnp.int32)[None]
    table = step_tables()
    raw_slots = raw.reshape(slots, 8, atoms)
    sums, away = descreen(dims, mask, flag, raw_slots, table)
    (born,) = exchange(
        born_kernel, 1, (sums.reshape(grid + (8, atoms)), raw),
        [grid + (1, atoms)], landing(rows_x, rows_y, 1) + [dma((2, 2, 5))],
    )
    moments, pair_sums = screen(dims, mask, raw_slots, born.reshape(slots, 1, atoms), table, away)
    shape = (rows_x, rows_y, atoms)
    return exchange(
        settle_kernel, 2,
        (moments.reshape(grid + (16, atoms)), pair_sums.reshape(grid + (16, atoms)), raw, born),
        [shape, shape, (3,) + shape, shape], landing(rows_x, rows_y, 8) + [dma((2, 5))],
    )


def solution(mesh):
    placed = (
        P(None, "gx", "gy", None),
        P("gx", "gy", None),
        P("gx", "gy", None),
        P(),
        P(),
        P("gx", "gy", None),
    )
    return jax.shard_map(
        body,
        mesh=mesh,
        in_specs=placed,
        out_specs=(
            P("gx", "gy", None),
            P("gx", "gy", None),
            P(None, "gx", "gy", None),
            P("gx", "gy", None),
        ),
        check_vma=False,
    )
```

```python
import functools

import jax
import jax.numpy as jnp
import numpy as np
from jax import lax
from jax.experimental import pallas as pl
from jax.experimental.pallas import tpu as pltpu
from jax.sharding import PartitionSpec as P

dielectric_factor = 1.0 - 1.0 / 78.5
radius_offset = 0.09
block_side = 8.0
log2e = 1.4426950408889634
ln2 = 0.6931471805599453
f32 = jnp.float32
bf16 = jnp.bfloat16

near_steps = ((0, 1), (1, -1), (1, 0), (1, 1))
far_steps = ((0, 2), (1, -2), (1, 2), (2, -2), (2, -1), (2, 0), (2, 1), (2, 2))
all_steps = near_steps + far_steps


def series_coefficients():
    top = (0.85 * 1.91 / 9.0) ** 2 * 1.001
    nodes = 0.5 * top * (1.0 + np.cos(np.pi * (np.arange(4) + 0.5) / 4))
    exact = sum(2.0 * (k + 1) / (2 * k + 3) * nodes**k for k in range(40))
    return [float(c) for c in np.polynomial.polynomial.polyfit(nodes, exact, 3)]


series = series_coefficients()
chunk = 64


def step_tables():
    scale = np.ones((13, 8))
    shift = np.zeros((13, 8))
    scale[12, 5:8] = 0.0
    for k, (ox, oy) in enumerate(all_steps):
        scale[k, 5:8] = (16 * ox, 16 * oy, 64 * (ox * ox + oy * oy))
        shift[k, 0:2] = (8 * ox, 8 * oy)
    none = np.zeros_like(shift)
    scale = np.concatenate([scale] * 6, axis=1)
    shift = np.concatenate([shift, none, shift, none, none, shift], axis=1)
    tables = np.stack([scale, shift])[..., None] * np.ones(128)
    return jnp.asarray(tables, bf16)


def split3(value):
    first = value.astype(bf16).astype(f32)
    rest = value - first
    second = rest.astype(bf16).astype(f32)
    return first, second, rest - second


def dot(a, b, ca, cb):
    return lax.dot_general(a, b, (((ca,), (cb,)), ((), ())), preferred_element_type=f32)


def sublane(shape=(8, 128)):
    return lax.broadcasted_iota(jnp.int32, shape, 0)


def squared_length(xyz):
    square = xyz * xyz
    return jnp.sum(square, axis=0, keepdims=True)


def centred(raw):
    row = sublane()
    middle = jnp.where(row < 2, 4.0, 8.0)
    return jnp.where(row < 3, raw - middle, 0.0)


def away_operand(xyz):
    length = squared_length(xyz)
    row = sublane()
    value = jnp.where(row < 3, xyz, jnp.where(row == 4, length, 1.0))
    value = jnp.where(row == 5, xyz[0:1], jnp.where(row == 6, xyz[1:2], value))
    step = jnp.where(row == 4, 2.0, 4.0)
    first = jnp.round(value * step) * (1.0 / step)
    rest = value - first
    second = rest.astype(bf16).astype(f32)
    third = rest - second
    return jnp.concatenate([first, second, first, second, third, first], axis=0).astype(bf16)


def home_operand(xyz, factor):
    length = squared_length(xyz)
    row = sublane()
    value = jnp.where(row < 3, -2.0 * xyz, jnp.where(row == 3, length, 1.0)) * factor
    first, second, third = split3(value)
    stacked = jnp.concatenate([first, first, second, second, first, third], axis=0)
    return jnp.transpose(stacked).astype(bf16)


def lanes_of(rows, k):
    return jnp.broadcast_to(rows[:, k : k + 1], (128, 128))


def fold(value):
    return jnp.sum(value.reshape(-1, 8, 128), axis=0)


def row_totals(value, eye):
    return fold(jnp.sum(value, axis=1, keepdims=True) * eye)


def close_integral(distance, quarter, log_factor, a, s, whole):
    outer = distance + s
    span = distance - s
    inner = jnp.maximum(jnp.abs(span) if whole else span, a)
    inner = jnp.minimum(inner, outer)
    inv_outer = 1.0 / outer
    inv_inner = 1.0 / inner
    ratio = outer * inv_inner
    total = (inv_inner - inv_outer) * (1.0 - (span * quarter) * (ratio + 1.0))
    total = total + log_factor * jnp.log2(ratio)
    if whole:
        total = total + 2.0 * (1.0 / a - 1.0 / jnp.maximum(a, -span))
    return total


def weave(*parts):
    live = list(parts)
    while live:
        for part in list(live):
            for _ in range(2 if part is parts[-1] and len(parts) > 1 else 1):
                if next(part, live) is live:
                    live.remove(part)
                    break


def descreen_kernel(
    dims, mask_ref, radius_ref, scale_ref, raw_ref, table_ref, out_ref, away_ref, near_ref, even_sq, odd_sq, even_cols, odd_cols, acc_ref
):
    rows_x, rows_y = dims
    width = rows_y + 4
    slots = (rows_x + 2) * width
    homes = rows_x * rows_y

    def prepare(slot):
        raw = raw_ref[slot]
        xyz = centred(raw)
        away_ref[slot] = away_operand(xyz)
        out_ref[slot] = jnp.zeros((8, 128), f32)
        s = raw[4:5]
        sq = s * s
        cube = s * sq
        near_ref[slot] = jnp.concatenate(
            [raw[3:5], series[0] * cube, series[1] * cube * sq, series[2] * cube * (sq * sq), series[3] * cube * (sq * sq) * sq, jnp.zeros((2, 128), f32)], axis=0
        )

    def prepare_turn(n, carry):
        for k in range(4):
            prepare(4 * n + k)
        return carry

    lax.fori_loop(0, slots // 4, prepare_turn, 0)
    eye = (
        lax.broadcasted_iota(jnp.int32, (128, 128), 0)
        == lax.broadcasted_iota(jnp.int32, (128, 128), 1)
    ).astype(f32)

    def slot_of(n):
        block_x = n // rows_y
        return block_x * width + 2 + (n - block_x * rows_y)

    def distances(n, sq_ref, cols_ref):
        slot = slot_of(n)
        left = home_operand(centred(raw_ref[slot]), 1.0)
        columns = jnp.transpose(near_ref[slot])
        sq_ref[:, 12 * 128 : 13 * 128] = dot(left, away_ref[slot] * table_ref[0, 12], 1, 0)
        cols_ref[0] = lanes_of(columns, 0)
        yield
        for k0 in range(0, 12, 2):
            right = []
            for k in (k0, k0 + 1):
                there = slot + all_steps[k][0] * width + all_steps[k][1]
                right.append(away_ref[there] * table_ref[0, k] + table_ref[1, k])
            sq_ref[:, 128 * k0 : 128 * k0 + 256] = dot(left, jnp.concatenate(right, axis=1), 1, 0)
            if k0 < 10:
                cols_ref[k0 // 2 + 1] = lanes_of(columns, k0 // 2 + 1)
            yield

    def pairs(n, sq_ref, cols_ref, whole):
        slot = slot_of(n)
        here = near_ref[slot]
        for c in range(0, 128, chunk):
            part = pl.ds(c, chunk)
            own = sq_ref[part, 12 * 128 : 13 * 128] + eye[c : c + chunk]
            inverse = lax.rsqrt(own)
            total = close_integral(own * inverse, 0.25 * inverse, (-0.5 * ln2) * inverse, cols_ref[0, part], here[1:2], whole)
            acc_ref[part] = total * (1.0 - eye[c : c + chunk])
        yield
        for k in range(12):
            there = slot + all_steps[k][0] * width + all_steps[k][1]
            ox, oy = all_steps[k]
            m = mask_ref[n * 25 + (ox + 2) * 5 + oy + 2].astype(f32)
            near = near_ref[there]
            backs = 0.0
            for c in range(0, 128, chunk):
                part = pl.ds(c, chunk)
                sq = sq_ref[part, 128 * k : 128 * k + 128]
                if k < 4:
                    inverse = lax.rsqrt(sq)
                    distance = sq * inverse
                    scales = (0.25 * inverse, (-0.5 * ln2) * inverse)
                    total = close_integral(distance, *scales, cols_ref[0, part], near[1:2] * m, whole)
                    back = close_integral(distance, *scales, near[0:1] + (1.0 - m) * 1e9, cols_ref[1, part], whole)
                else:
                    rows = near * m
                    w = 1.0 / sq
                    ww = w * w
                    total = ww * (rows[2:3] + w * (rows[3:4] + w * (rows[4:5] + w * rows[5:6])))
                    back = ww * (cols_ref[2, part] + w * (cols_ref[3, part] + w * (cols_ref[4, part] + w * cols_ref[5, part])))
                acc_ref[part] += total
                backs = backs + fold(back)
            out_ref[there] += backs if k < 4 else m * backs
            yield
        out_ref[slot] += row_totals(acc_ref[...], eye)
        yield

    def turns(whole):
        weave(distances(0, even_sq, even_cols))

        def turn(i, carry):
            n = 2 * i
            weave(distances(n + 1, odd_sq, odd_cols), pairs(n, even_sq, even_cols, whole))
            weave(
                distances(jnp.minimum(n + 2, homes - 1), even_sq, even_cols),
                pairs(n + 1, odd_sq, odd_cols, whole),
            )
            return carry

        lax.fori_loop(0, homes // 2, turn, 0)

    least, most = radius_ref[0] - radius_offset, 0.0
    for k in range(radius_ref.shape[0]):
        inner = radius_ref[k] - radius_offset
        least = jnp.minimum(least, inner)
        most = jnp.maximum(most, scale_ref[k] * inner)
    reached = most - 0.99 > least

    @pl.when(jnp.logical_not(reached))
    def _():
        turns(False)

    @pl.when(reached)
    def _():
        turns(True)


def screen_kernel(
    dims, mask_ref, raw_ref, born_ref, table_ref, away_ref, moment_ref, out_ref, rows_ref, vec_ref,
    even_sq, odd_sq, even_cols, odd_cols, even_high, odd_high, even_low, odd_low, acc_ref,
):
    rows_x, rows_y = dims
    width = rows_y + 4
    slots = (rows_x + 2) * width
    homes = rows_x * rows_y

    def prepare(slot):
        raw = raw_ref[slot]
        xyz = centred(raw)
        born = born_ref[slot]
        inv = 1.0 / born
        half = lax.rsqrt(born)
        charge = raw[5:6]
        weak = charge * half
        strong = weak * inv
        block_x = slot // width
        block_y = slot - block_x * width
        x = xyz[0:1] + 8.0 * (block_x.astype(f32) - 0.5 * (rows_x + 1))
        y = xyz[1:2] + 8.0 * (block_y.astype(f32) - 0.5 * (width - 1))
        vector = jnp.concatenate([strong, strong * x, strong * y, strong * xyz[2:3]], axis=0)
        first, second, third = split3(vector)
        vec_ref[slot] = jnp.concatenate([first, second, third, jnp.zeros((4, 128), f32)], axis=0).astype(bf16)
        rows_ref[slot] = jnp.concatenate([inv, -log2e * inv, weak, jnp.zeros((5, 128), f32)], axis=0)
        out_ref[slot] = jnp.zeros((16, 128), f32)
        moment_ref[slot] = jnp.zeros((16, 128), f32)

    def prepare_turn(n, carry):
        for k in range(4):
            prepare(4 * n + k)
        return carry

    lax.fori_loop(0, slots // 4, prepare_turn, 0)
    odd_high[...] = jnp.zeros_like(odd_high)
    odd_low[...] = jnp.zeros_like(odd_low)
    eye = (
        lax.broadcasted_iota(jnp.int32, (128, 128), 0)
        == lax.broadcasted_iota(jnp.int32, (128, 128), 1)
    ).astype(f32)

    def pair_terms(scaled_sq, rows):
        t = scaled_sq * rows[0:1]
        e = 0.25 * jnp.exp2(scaled_sq * rows[1:2])
        inv = lax.rsqrt(t + e)
        cube = inv * inv * inv
        damped = e * cube
        return inv, cube - damped, damped + damped * t

    def slot_of(n):
        block_x = n // rows_y
        return block_x * width + 2 + (n - block_x * rows_y)

    def mask_of(n, k):
        ox, oy = all_steps[k]
        return mask_ref[n * 25 + (ox + 2) * 5 + oy + 2].astype(f32)

    def away_of(slot, k):
        return slot + all_steps[k][0] * width + all_steps[k][1]

    def distances(n, sq_ref, cols_ref):
        slot = slot_of(n)
        here = rows_ref[slot]
        left = home_operand(centred(raw_ref[slot]), 0.25 * here[0:1])
        cols_ref[...] = lanes_of(jnp.transpose(here), 2)
        sq_ref[:, 12 * 128 : 13 * 128] = dot(left, away_ref[slot] * table_ref[0, 12], 1, 0)
        yield
        for k0 in range(0, 12, 2):
            right = [away_ref[away_of(slot, k)] * table_ref[0, k] + table_ref[1, k] for k in (k0, k0 + 1)]
            sq_ref[:, 128 * k0 : 128 * k0 + 256] = dot(left, jnp.concatenate(right, axis=1), 1, 0)
            yield

    def pairs(n, sq_ref, cols_ref, high_ref, low_ref):
        slot = slot_of(n)
        here = rows_ref[slot]

        def keep(part, k, pull):
            high = pull.astype(bf16)
            high_ref[part, 128 * k : 128 * k + 128] = high
            low_ref[part, 128 * k : 128 * k + 128] = (pull - high.astype(f32)).astype(bf16)

        for c in range(0, 128, chunk):
            part = pl.ds(c, chunk)
            inv, pull, stretch = pair_terms(sq_ref[part, 12 * 128 : 13 * 128], here)
            off = 1.0 - eye[c : c + chunk]
            weak = off * here[2:3]
            acc_ref[0, part] = inv * weak
            acc_ref[1, part] = stretch * weak
            keep(part, 12, pull * off)
        yield
        for k in range(12):
            there = away_of(slot, k)
            rows = rows_ref[there]
            m = mask_of(n, k)
            weak = rows[2:3] * m
            near, far = 0.0, 0.0
            for c in range(0, 128, chunk):
                part = pl.ds(c, chunk)
                inv, pull, stretch = pair_terms(sq_ref[part, 128 * k : 128 * k + 128], rows)
                acc_ref[0, part] += inv * weak
                acc_ref[1, part] += stretch * weak
                near = near + fold(inv * cols_ref[part])
                far = far + fold(stretch * cols_ref[part])
                keep(part, k, pull)
            out_ref[there, 0:8] += m * near
            out_ref[there, 8:16] += m * far
            yield
        out_ref[slot, 0:8] += row_totals(acc_ref[0], eye)
        out_ref[slot, 8:16] += row_totals(acc_ref[1], eye)
        yield

    def moments(n, high_ref, low_ref):
        slot = slot_of(n)
        own = vec_ref[slot]
        own = jnp.concatenate([own, own], axis=1)
        vectors = [vec_ref[away_of(slot, k)] * mask_of(n, k).astype(bf16) for k in range(12)] + [vec_ref[slot]]
        totals = 0.0
        for k0 in range(0, 12, 2):
            lanes = slice(128 * k0, 128 * k0 + 256)
            back = dot(own, jnp.concatenate([high_ref[:, lanes], low_ref[:, lanes]], axis=0), 1, 0)
            for t in range(2):
                moment_ref[away_of(slot, k0 + t)] += mask_of(n, k0 + t) * back[:, 128 * t : 128 * t + 128]
            group = slice(k0, k0 + 3 if k0 == 10 else k0 + 2)
            lanes = slice(128 * group.start, 128 * group.stop)
            totals = totals + dot(
                jnp.concatenate([high_ref[:, lanes], low_ref[:, lanes]], axis=1),
                jnp.concatenate(vectors[group] * 2, axis=1), 1, 1,
            )
            yield
        moment_ref[slot] += jnp.transpose(totals)
        yield

    weave(distances(0, even_sq, even_cols))

    def turn(i, carry):
        for n in [16 * i + 2 * u for u in range(8)]:
            weave(
                distances(n + 1, odd_sq, odd_cols),
                moments(jnp.maximum(n - 1, 0), odd_high, odd_low),
                pairs(n, even_sq, even_cols, even_high, even_low),
            )
            weave(
                distances(jnp.minimum(n + 2, homes - 1), even_sq, even_cols),
                moments(n, even_high, even_low),
                pairs(n + 1, odd_sq, odd_cols, odd_high, odd_low),
            )
        return carry

    lax.fori_loop(0, homes // 16, turn, 0)
    weave(moments(homes - 1, odd_high, odd_low))


def descreen(dims, mask, type_radius, type_scale, raw, table):
    slots = raw.shape[0]
    smem = pl.BlockSpec(memory_space=pltpu.SMEM)
    vmem = pl.BlockSpec(memory_space=pltpu.VMEM)
    return pl.pallas_call(
        functools.partial(descreen_kernel, dims),
        out_shape=(
            jax.ShapeDtypeStruct((slots, 8, 128), f32),
            jax.ShapeDtypeStruct((slots, 48, 128), bf16),
        ),
        in_specs=[smem, smem, smem, vmem, vmem],
        out_specs=(vmem, vmem),
        scratch_shapes=[
            pltpu.VMEM((slots, 8, 128), f32),
            pltpu.VMEM((128, 13 * 128), f32),
            pltpu.VMEM((128, 13 * 128), f32),
            pltpu.VMEM((6, 128, 128), f32),
            pltpu.VMEM((6, 128, 128), f32),
            pltpu.VMEM((128, 128), f32),
        ],
        compiler_params=pltpu.CompilerParams(vmem_limit_bytes=56 * 2**20),
        name="descreen",
    )(mask, type_radius, type_scale, raw, table)


def screen(dims, mask, raw, born, table, away):
    slots = raw.shape[0]
    smem = pl.BlockSpec(memory_space=pltpu.SMEM)
    vmem = pl.BlockSpec(memory_space=pltpu.VMEM)
    return pl.pallas_call(
        functools.partial(screen_kernel, dims),
        out_shape=(
            jax.ShapeDtypeStruct((slots, 16, 128), f32),
            jax.ShapeDtypeStruct((slots, 16, 128), f32),
        ),
        in_specs=[smem, vmem, vmem, vmem, vmem],
        out_specs=(vmem, vmem),
        scratch_shapes=[
            pltpu.VMEM((slots, 8, 128), f32),
            pltpu.VMEM((slots, 16, 128), bf16),
            pltpu.VMEM((128, 13 * 128), f32),
            pltpu.VMEM((128, 13 * 128), f32),
            pltpu.VMEM((128, 128), f32),
            pltpu.VMEM((128, 128), f32),
            pltpu.VMEM((128, 13 * 128), bf16),
            pltpu.VMEM((128, 13 * 128), bf16),
            pltpu.VMEM((128, 13 * 128), bf16),
            pltpu.VMEM((128, 13 * 128), bf16),
            pltpu.VMEM((2, 128, 128), f32),
        ],
        compiler_params=pltpu.CompilerParams(vmem_limit_bytes=56 * 2**20),
        name="screen",
    )(mask, raw, born, table, away)


def around(dx, dy):
    count_x, count_y = lax.axis_size("gx"), lax.axis_size("gy")
    return (
        lax.rem(lax.axis_index("gx") + (dx + count_x), count_x),
        lax.rem(lax.axis_index("gy") + (dy + count_y), count_y),
    )


def greet():
    barrier = pltpu.get_barrier_semaphore()
    ring = [(dx, dy) for dx in (-1, 0, 1) for dy in (-1, 0, 1) if (dx, dy) != (0, 0)]
    for dx, dy in ring:
        pl.semaphore_signal(barrier, inc=1, device_id=around(dx, dy), device_id_type=pl.DeviceIdType.MESH)
    pl.semaphore_wait(barrier, len(ring))


def send(src, dst, sems, k, to):
    copy = pltpu.make_async_remote_copy(
        src_ref=src,
        dst_ref=dst,
        send_sem=sems.at[0, k],
        recv_sem=sems.at[1, k],
        device_id=around(*to),
        device_id_type=pl.DeviceIdType.MESH,
    )
    copy.start()
    return copy


def fill_halo(ext, sems, rows_x, rows_y):
    own = pl.ds(2, rows_y)
    top, ahead = pl.ds(0, 2), pl.ds(rows_x, 2)
    body_rows = pl.ds(0, rows_x)
    left, first = pl.ds(0, 2), pl.ds(2, 2)
    last, right = pl.ds(rows_y, 2), pl.ds(rows_y + 2, 2)
    plan = [
        (top, own, ahead, own, (-1, 0)),
        (body_rows, last, body_rows, left, (0, 1)),
        (body_rows, first, body_rows, right, (0, -1)),
        (top, last, ahead, left, (-1, 1)),
        (top, first, ahead, right, (-1, -1)),
    ]
    copies = [
        send(ext.at[rs, cs], ext.at[rd, cd], sems, k, to)
        for k, (rs, cs, rd, cd, to) in enumerate(plan)
    ]
    for copy in copies:
        copy.wait()


def give_back(ext, ahead_land, side_land, corner_land, sems, rows_x, rows_y):
    own = pl.ds(2, rows_y)
    ahead, body_rows = pl.ds(rows_x, 2), pl.ds(0, rows_x)
    left, right = pl.ds(0, 2), pl.ds(rows_y + 2, 2)
    copies = [
        send(ext.at[ahead, own], ahead_land, sems, 0, (1, 0)),
        send(ext.at[body_rows, left], side_land.at[0], sems, 1, (0, -1)),
        send(ext.at[body_rows, right], side_land.at[1], sems, 2, (0, 1)),
        send(ext.at[ahead, left], corner_land.at[0], sems, 3, (1, -1)),
        send(ext.at[ahead, right], corner_land.at[1], sems, 4, (1, 1)),
    ]
    for copy in copies:
        copy.wait()
    ext[0:2, 2 : rows_y + 2] += ahead_land[...]
    ext[0:rows_x, rows_y : rows_y + 2] += side_land[0]
    ext[0:rows_x, 2:4] += side_land[1]
    ext[0:2, rows_y : rows_y + 2] += corner_land[0]
    ext[0:2, 2:4] += corner_land[1]


def gather_kernel(radius_ref, scale_ref, offsets_ref, charge_ref, type_ref, ext, sems):
    rows_x, rows_y, _ = charge_ref.shape
    greet()
    for x in range(rows_x):
        for y in range(0, rows_y, 8):
            types = type_ref[x, y : y + 8]
            radius = jnp.zeros((8, 128), f32)
            scale = jnp.zeros((8, 128), f32)
            for k in range(radius_ref.shape[0]):
                radius = jnp.where(types == k, radius_ref[k], radius)
                scale = jnp.where(types == k, scale_ref[k], scale)
            inner = radius - radius_offset
            parts = [offsets_ref[k, x, y : y + 8] for k in range(3)]
            parts += [inner, scale * inner, charge_ref[x, y : y + 8], radius, jnp.zeros((8, 128), f32)]
            for k, part in enumerate(parts):
                ext[x, 2 + y : 10 + y, k, :] = part
    fill_halo(ext, sems, rows_x, rows_y)


def born_kernel(sum_ref, raw_ref, born_ref, ext, ahead_land, side_land, corner_land, sems):
    width = sum_ref.shape[1]
    rows_x, rows_y = sum_ref.shape[0] - 2, width - 4
    greet()

    def reduce_turn(x, carry):
        for y in range(width):
            ext[x, y] = jnp.sum(sum_ref[x, y], axis=0, keepdims=True)
        return carry

    lax.fori_loop(0, rows_x + 2, reduce_turn, 0)
    give_back(ext, ahead_land, side_land, corner_land, sems.at[0], rows_x, rows_y)

    def radius_turn(x, carry):
        for y in range(2, rows_y + 2):
            raw = raw_ref[x, y]
            inner, radius = raw[3:4], raw[6:7]
            psi = 0.5 * inner * ext[x, y]
            bent = jnp.tanh(psi * (1.0 - 0.8 * psi + 4.85 * psi * psi))
            born_ref[x, y] = 1.0 / (1.0 / inner - bent / radius)
        return carry

    lax.fori_loop(0, rows_x, radius_turn, 0)
    fill_halo(born_ref, sems.at[1], rows_x, rows_y)


def settle_kernel(
    moment_ref, sum_ref, raw_ref, born_ref, ext, ahead_land, side_land, corner_land, sems
):
    width = sum_ref.shape[1]
    rows_x, rows_y = sum_ref.shape[0] - 2, width - 4
    greet()
    row = sublane()

    def finish_turn(x, carry):
        for y in range(width):
            raw = raw_ref[x, y]
            born = born_ref[x, y]
            inv = 1.0 / born
            weak = raw[5:6] * lax.rsqrt(born)
            strong = weak * inv
            moment = moment_ref[x, y]
            moment = moment[0:8] + moment[8:16]
            moment = moment[0:4] + moment[4:8]
            middle = jnp.where(row == 0, 8.0 * (x.astype(f32) - 0.5 * (rows_x + 1)) - 4.0, 8.0 * (y - 0.5 * (width - 1)) - 4.0)
            place = raw + jnp.where(row == 2, -8.0, middle)
            force = ((-dielectric_factor / 8.0) * strong) * (place[0:3] * moment[0:1] - moment[1:4])
            sums = sum_ref[x, y]
            energy = ((-0.25 * dielectric_factor) * weak) * jnp.sum(sums[0:8], axis=0, keepdims=True)
            grad = ((0.25 * dielectric_factor) * strong) * jnp.sum(sums[8:16], axis=0, keepdims=True)
            ext[x, y] = jnp.concatenate([force, energy, grad, jnp.zeros((3, 128), f32)], axis=0)
        return carry

    lax.fori_loop(0, rows_x + 2, finish_turn, 0)
    give_back(ext, ahead_land, side_land, corner_land, sems, rows_x, rows_y)


def finish_kernel(ext, raw_ref, born_ref, born_out, energy_out, force_out, grad_out):
    rows_x, rows_y, _ = born_out.shape
    for x in range(rows_x):
        for y in range(0, rows_y, 8):
            here = slice(2 + y, 10 + y)
            there = slice(y, y + 8)
            born = born_ref[x, here, 0, :]
            charge = raw_ref[x, here, 5, :]
            own = (0.5 * dielectric_factor) * (charge * charge) / born
            born_out[x, there] = born
            for k in range(3):
                force_out[k, x, there] = ext[x, here, k, :]
            energy_out[x, there] = ext[x, here, 3, :] - own
            grad_out[x, there] = ext[x, here, 4, :] + own / born


def exchange(kernel, ident, ins, outs, scratch):
    smem = pl.BlockSpec(memory_space=pltpu.SMEM)
    vmem = pl.BlockSpec(memory_space=pltpu.VMEM)
    return pl.pallas_call(
        kernel,
        out_shape=tuple(jax.ShapeDtypeStruct(shape, f32) for shape in outs),
        in_specs=[smem if value.ndim == 1 else vmem for value in ins],
        out_specs=tuple(vmem for _ in outs),
        scratch_shapes=scratch,
        compiler_params=pltpu.CompilerParams(
            collective_id=ident, has_side_effects=ident is not None, vmem_limit_bytes=56 * 2**20
        ),
        name=kernel.__name__,
    )(*ins)


def landing(rows_x, rows_y, depth):
    return [
        pltpu.VMEM((rows_x + 2, rows_y + 4, depth, 128), f32),
        pltpu.VMEM((2, rows_y, depth, 128), f32),
        pltpu.VMEM((2, rows_x, 2, depth, 128), f32),
        pltpu.VMEM((2, 2, 2, depth, 128), f32),
    ]


def body(offsets, charges, atom_type, type_radius, type_scale, tile_mask):
    rows_x, rows_y, atoms = charges.shape
    dims = (rows_x, rows_y)
    grid = (rows_x + 2, rows_y + 4)
    slots = grid[0] * grid[1]
    dma = pltpu.SemaphoreType.DMA
    (raw,) = exchange(
        gather_kernel, 0, (type_radius, type_scale, offsets, charges, atom_type),
        [grid + (8, atoms)], [dma((2, 5))],
    )
    mask = tile_mask.reshape(-1)
    table = step_tables()
    raw_slots = raw.reshape(slots, 8, atoms)
    sums, away = descreen(dims, mask, type_radius, type_scale, raw_slots, table)
    (born,) = exchange(
        born_kernel, 1, (sums.reshape(grid + (8, atoms)), raw),
        [grid + (1, atoms)], landing(rows_x, rows_y, 1) + [dma((2, 2, 5))],
    )
    moments, pair_sums = screen(dims, mask, raw_slots, born.reshape(slots, 1, atoms), table, away)
    (settled,) = exchange(
        settle_kernel, 2,
        (moments.reshape(grid + (16, atoms)), pair_sums.reshape(grid + (16, atoms)), raw, born),
        [grid + (8, atoms)], landing(rows_x, rows_y, 8)[1:] + [dma((2, 5))],
    )
    shape = (rows_x, rows_y, atoms)
    return exchange(
        finish_kernel, None, (settled, raw, born), [shape, shape, (3,) + shape, shape], []
    )


def solution(mesh):
    placed = (
        P(None, "gx", "gy", None),
        P("gx", "gy", None),
        P("gx", "gy", None),
        P(),
        P(),
        P("gx", "gy", None),
    )
    return jax.shard_map(
        body,
        mesh=mesh,
        in_specs=placed,
        out_specs=(
            P("gx", "gy", None),
            P("gx", "gy", None),
            P(None, "gx", "gy", None),
            P("gx", "gy", None),
        ),
        check_vma=False,
    )
```

```python
import functools

import jax
import jax.numpy as jnp
import numpy as np
from jax import lax
from jax.experimental import pallas as pl
from jax.experimental.pallas import tpu as pltpu
from jax.sharding import PartitionSpec as P

dielectric_factor = 1.0 - 1.0 / 78.5
radius_offset = 0.09
block_side = 8.0
log2e = 1.4426950408889634
ln2 = 0.6931471805599453
f32 = jnp.float32
bf16 = jnp.bfloat16

near_steps = ((0, 1), (1, -1), (1, 0), (1, 1))
far_steps = ((0, 2), (1, -2), (1, 2), (2, -2), (2, -1), (2, 0), (2, 1), (2, 2))
all_steps = near_steps + far_steps


def series_coefficients():
    top = (0.85 * 1.91 / 9.0) ** 2 * 1.001
    nodes = 0.5 * top * (1.0 + np.cos(np.pi * (np.arange(4) + 0.5) / 4))
    exact = sum(2.0 * (k + 1) / (2 * k + 3) * nodes**k for k in range(40))
    return [float(c) for c in np.polynomial.polynomial.polyfit(nodes, exact, 3)]


series = series_coefficients()
chunk = 64


def step_tables():
    scale = np.ones((13, 8))
    shift = np.zeros((13, 8))
    scale[12, 5:8] = 0.0
    for k, (ox, oy) in enumerate(all_steps):
        scale[k, 5:8] = (16 * ox, 16 * oy, 64 * (ox * ox + oy * oy))
        shift[k, 0:2] = (8 * ox, 8 * oy)
    none = np.zeros_like(shift)
    scale = np.concatenate([scale] * 6, axis=1)
    shift = np.concatenate([shift, none, shift, none, none, shift], axis=1)
    tables = np.stack([scale, shift])[..., None] * np.ones(128)
    return jnp.asarray(tables, bf16)


def split3(value):
    first = value.astype(bf16).astype(f32)
    rest = value - first
    second = rest.astype(bf16).astype(f32)
    return first, second, rest - second


def dot(a, b, ca, cb):
    return lax.dot_general(a, b, (((ca,), (cb,)), ((), ())), preferred_element_type=f32)


def sublane(shape=(8, 128)):
    return lax.broadcasted_iota(jnp.int32, shape, 0)


def squared_length(xyz):
    square = xyz * xyz
    return jnp.sum(square, axis=0, keepdims=True)


def centred(raw):
    row = sublane()
    middle = jnp.where(row < 2, 4.0, 8.0)
    return jnp.where(row < 3, raw - middle, 0.0)


def away_operand(xyz):
    length = squared_length(xyz)
    row = sublane()
    value = jnp.where(row < 3, xyz, jnp.where(row == 4, length, 1.0))
    value = jnp.where(row == 5, xyz[0:1], jnp.where(row == 6, xyz[1:2], value))
    step = jnp.where(row == 4, 2.0, 4.0)
    first = jnp.round(value * step) * (1.0 / step)
    rest = value - first
    second = rest.astype(bf16).astype(f32)
    third = rest - second
    return jnp.concatenate([first, second, first, second, third, first], axis=0).astype(bf16)


def home_operand(xyz, factor):
    length = squared_length(xyz)
    row = sublane()
    value = jnp.where(row < 3, -2.0 * xyz, jnp.where(row == 3, length, 1.0)) * factor
    first, second, third = split3(value)
    stacked = jnp.concatenate([first, first, second, second, first, third], axis=0)
    return jnp.transpose(stacked).astype(bf16)


def lanes_of(rows, k):
    return jnp.broadcast_to(rows[:, k : k + 1], (128, 128))


def fold(value):
    return jnp.sum(value.reshape(-1, 8, 128), axis=0)


def row_totals(value, eye):
    return fold(jnp.sum(value, axis=1, keepdims=True) * eye)


def close_integral(distance, quarter, log_factor, a, s, whole):
    outer = distance + s
    span = distance - s
    inner = jnp.maximum(jnp.abs(span) if whole else span, a)
    inner = jnp.minimum(inner, outer)
    inv_outer = 1.0 / outer
    inv_inner = 1.0 / inner
    ratio = outer * inv_inner
    total = (inv_inner - inv_outer) * (1.0 - (span * quarter) * (ratio + 1.0))
    total = total + log_factor * jnp.log2(ratio)
    if whole:
        total = total + 2.0 * (1.0 / a - 1.0 / jnp.maximum(a, -span))
    return total


def weave(*parts):
    live = list(parts)
    while live:
        for part in list(live):
            for _ in range(2 if part is parts[-1] and len(parts) > 1 else 1):
                if next(part, live) is live:
                    live.remove(part)
                    break


def descreen_kernel(
    dims, mask_ref, radius_ref, scale_ref, raw_ref, table_ref, out_ref, away_ref, near_ref, even_sq, odd_sq, even_cols, odd_cols, acc_ref
):
    rows_x, rows_y = dims
    width = rows_y + 4
    slots = (rows_x + 2) * width
    homes = rows_x * rows_y

    def prepare(slot):
        raw = raw_ref[slot]
        xyz = centred(raw)
        away_ref[slot] = away_operand(xyz)
        out_ref[slot] = jnp.zeros((8, 128), f32)
        s = raw[4:5]
        sq = s * s
        cube = s * sq
        near_ref[slot] = jnp.concatenate(
            [raw[3:5], series[0] * cube, series[1] * cube * sq, series[2] * cube * (sq * sq), series[3] * cube * (sq * sq) * sq, jnp.zeros((2, 128), f32)], axis=0
        )

    def prepare_turn(n, carry):
        for k in range(4):
            prepare(4 * n + k)
        return carry

    lax.fori_loop(0, slots // 4, prepare_turn, 0)
    eye = (
        lax.broadcasted_iota(jnp.int32, (128, 128), 0)
        == lax.broadcasted_iota(jnp.int32, (128, 128), 1)
    ).astype(f32)

    def slot_of(n):
        block_x = n // rows_y
        return block_x * width + 2 + (n - block_x * rows_y)

    def distances(n, sq_ref, cols_ref):
        slot = slot_of(n)
        left = home_operand(centred(raw_ref[slot]), 1.0)
        columns = jnp.transpose(near_ref[slot])
        sq_ref[:, 12 * 128 : 13 * 128] = dot(left, away_ref[slot] * table_ref[0, 12], 1, 0)
        cols_ref[0] = lanes_of(columns, 0)
        yield
        for k0 in range(0, 12, 2):
            right = []
            for k in (k0, k0 + 1):
                there = slot + all_steps[k][0] * width + all_steps[k][1]
                right.append(away_ref[there] * table_ref[0, k] + table_ref[1, k])
            sq_ref[:, 128 * k0 : 128 * k0 + 256] = dot(left, jnp.concatenate(right, axis=1), 1, 0)
            if k0 < 10:
                cols_ref[k0 // 2 + 1] = lanes_of(columns, k0 // 2 + 1)
            yield

    def pairs(n, sq_ref, cols_ref, whole):
        slot = slot_of(n)
        here = near_ref[slot]
        for c in range(0, 128, chunk):
            part = pl.ds(c, chunk)
            own = sq_ref[part, 12 * 128 : 13 * 128] + eye[c : c + chunk]
            inverse = lax.rsqrt(own)
            total = close_integral(own * inverse, 0.25 * inverse, (-0.5 * ln2) * inverse, cols_ref[0, part], here[1:2], whole)
            acc_ref[part] = total * (1.0 - eye[c : c + chunk])
        yield
        for k in range(12):
            there = slot + all_steps[k][0] * width + all_steps[k][1]
            ox, oy = all_steps[k]
            m = mask_ref[n * 25 + (ox + 2) * 5 + oy + 2].astype(f32)
            near = near_ref[there]
            backs = 0.0
            for c in range(0, 128, chunk):
                part = pl.ds(c, chunk)
                sq = sq_ref[part, 128 * k : 128 * k + 128]
                if k < 4:
                    inverse = lax.rsqrt(sq)
                    distance = sq * inverse
                    scales = (0.25 * inverse, (-0.5 * ln2) * inverse)
                    total = close_integral(distance, *scales, cols_ref[0, part], near[1:2] * m, whole)
                    back = close_integral(distance, *scales, near[0:1] + (1.0 - m) * 1e9, cols_ref[1, part], whole)
                else:
                    rows = near * m
                    w = 1.0 / sq
                    ww = w * w
                    total = ww * (rows[2:3] + w * (rows[3:4] + w * (rows[4:5] + w * rows[5:6])))
                    back = ww * (cols_ref[2, part] + w * (cols_ref[3, part] + w * (cols_ref[4, part] + w * cols_ref[5, part])))
                acc_ref[part] += total
                backs = backs + fold(back)
            out_ref[there] += backs if k < 4 else m * backs
            yield
        out_ref[slot] += row_totals(acc_ref[...], eye)
        yield

    def turns(whole):
        weave(distances(0, even_sq, even_cols))

        def turn(i, carry):
            n = 2 * i
            weave(distances(n + 1, odd_sq, odd_cols), pairs(n, even_sq, even_cols, whole))
            weave(
                distances(jnp.minimum(n + 2, homes - 1), even_sq, even_cols),
                pairs(n + 1, odd_sq, odd_cols, whole),
            )
            return carry

        lax.fori_loop(0, homes // 2, turn, 0)

    least, most = radius_ref[0] - radius_offset, 0.0
    for k in range(radius_ref.shape[0]):
        inner = radius_ref[k] - radius_offset
        least = jnp.minimum(least, inner)
        most = jnp.maximum(most, scale_ref[k] * inner)
    reached = most - 0.99 > least

    @pl.when(jnp.logical_not(reached))
    def _():
        turns(False)

    @pl.when(reached)
    def _():
        turns(True)


def screen_kernel(
    dims, mask_ref, raw_ref, born_ref, table_ref, away_ref, moment_ref, out_ref, rows_ref, vec_ref,
    even_sq, odd_sq, even_cols, odd_cols, even_high, odd_high, even_low, odd_low, acc_ref,
):
    rows_x, rows_y = dims
    width = rows_y + 4
    slots = (rows_x + 2) * width
    homes = rows_x * rows_y

    def prepare(slot):
        raw = raw_ref[slot]
        xyz = centred(raw)
        born = born_ref[slot]
        inv = 1.0 / born
        half = lax.rsqrt(born)
        charge = raw[5:6]
        weak = charge * half
        strong = weak * inv
        block_x = slot // width
        block_y = slot - block_x * width
        x = xyz[0:1] + 8.0 * (block_x.astype(f32) - 0.5 * (rows_x + 1))
        y = xyz[1:2] + 8.0 * (block_y.astype(f32) - 0.5 * (width - 1))
        vector = jnp.concatenate([strong, strong * x, strong * y, strong * xyz[2:3]], axis=0)
        first, second, third = split3(vector)
        vec_ref[slot] = jnp.concatenate([first, second, third, jnp.zeros((4, 128), f32)], axis=0).astype(bf16)
        rows_ref[slot] = jnp.concatenate([inv, -log2e * inv, weak, jnp.zeros((5, 128), f32)], axis=0)
        out_ref[slot] = jnp.zeros((16, 128), f32)
        moment_ref[slot] = jnp.zeros((16, 128), f32)

    def prepare_turn(n, carry):
        for k in range(4):
            prepare(4 * n + k)
        return carry

    lax.fori_loop(0, slots // 4, prepare_turn, 0)
    odd_high[...] = jnp.zeros_like(odd_high)
    odd_low[...] = jnp.zeros_like(odd_low)
    eye = (
        lax.broadcasted_iota(jnp.int32, (128, 128), 0)
        == lax.broadcasted_iota(jnp.int32, (128, 128), 1)
    ).astype(f32)

    def pair_terms(scaled_sq, rows):
        t = scaled_sq * rows[0:1]
        e = 0.25 * jnp.exp2(scaled_sq * rows[1:2])
        inv = lax.rsqrt(t + e)
        cube = inv * inv * inv
        damped = e * cube
        return inv, cube - damped, damped + damped * t

    def slot_of(n):
        block_x = n // rows_y
        return block_x * width + 2 + (n - block_x * rows_y)

    def mask_of(n, k):
        ox, oy = all_steps[k]
        return mask_ref[n * 25 + (ox + 2) * 5 + oy + 2].astype(f32)

    def away_of(slot, k):
        return slot + all_steps[k][0] * width + all_steps[k][1]

    def distances(n, sq_ref, cols_ref):
        slot = slot_of(n)
        here = rows_ref[slot]
        left = home_operand(centred(raw_ref[slot]), 0.25 * here[0:1])
        cols_ref[...] = lanes_of(jnp.transpose(here), 2)
        sq_ref[:, 12 * 128 : 13 * 128] = dot(left, away_ref[slot] * table_ref[0, 12], 1, 0)
        yield
        for k0 in range(0, 12, 2):
            right = [away_ref[away_of(slot, k)] * table_ref[0, k] + table_ref[1, k] for k in (k0, k0 + 1)]
            sq_ref[:, 128 * k0 : 128 * k0 + 256] = dot(left, jnp.concatenate(right, axis=1), 1, 0)
            yield

    def pairs(n, sq_ref, cols_ref, high_ref, low_ref):
        slot = slot_of(n)
        here = rows_ref[slot]

        def keep(part, k, pull):
            high = pull.astype(bf16)
            high_ref[part, 128 * k : 128 * k + 128] = high
            low_ref[part, 128 * k : 128 * k + 128] = (pull - high.astype(f32)).astype(bf16)

        for c in range(0, 128, chunk):
            part = pl.ds(c, chunk)
            inv, pull, stretch = pair_terms(sq_ref[part, 12 * 128 : 13 * 128], here)
            off = 1.0 - eye[c : c + chunk]
            weak = off * here[2:3]
            acc_ref[0, part] = inv * weak
            acc_ref[1, part] = stretch * weak
            keep(part, 12, pull * off)
        yield
        for k in range(12):
            there = away_of(slot, k)
            rows = rows_ref[there]
            m = mask_of(n, k)
            weak = rows[2:3] * m
            near, far = 0.0, 0.0
            for c in range(0, 128, chunk):
                part = pl.ds(c, chunk)
                inv, pull, stretch = pair_terms(sq_ref[part, 128 * k : 128 * k + 128], rows)
                acc_ref[0, part] += inv * weak
                acc_ref[1, part] += stretch * weak
                near = near + fold(inv * cols_ref[part])
                far = far + fold(stretch * cols_ref[part])
                keep(part, k, pull)
            out_ref[there, 0:8] += m * near
            out_ref[there, 8:16] += m * far
            yield
        out_ref[slot, 0:8] += row_totals(acc_ref[0], eye)
        out_ref[slot, 8:16] += row_totals(acc_ref[1], eye)
        yield

    def moments(n, high_ref, low_ref):
        slot = slot_of(n)
        own = vec_ref[slot]
        own = jnp.concatenate([own, own], axis=1)
        vectors = [vec_ref[away_of(slot, k)] * mask_of(n, k).astype(bf16) for k in range(12)] + [vec_ref[slot]]
        totals = 0.0
        for k0 in range(0, 12, 2):
            lanes = slice(128 * k0, 128 * k0 + 256)
            back = dot(own, jnp.concatenate([high_ref[:, lanes], low_ref[:, lanes]], axis=0), 1, 0)
            for t in range(2):
                moment_ref[away_of(slot, k0 + t)] += mask_of(n, k0 + t) * back[:, 128 * t : 128 * t + 128]
            group = slice(k0, k0 + 3 if k0 == 10 else k0 + 2)
            lanes = slice(128 * group.start, 128 * group.stop)
            totals = totals + dot(
                jnp.concatenate([high_ref[:, lanes], low_ref[:, lanes]], axis=1),
                jnp.concatenate(vectors[group] * 2, axis=1), 1, 1,
            )
            yield
        moment_ref[slot] += jnp.transpose(totals)
        yield

    weave(distances(0, even_sq, even_cols))

    def turn(i, carry):
        for n in [16 * i + 2 * u for u in range(8)]:
            weave(
                distances(n + 1, odd_sq, odd_cols),
                moments(jnp.maximum(n - 1, 0), odd_high, odd_low),
                pairs(n, even_sq, even_cols, even_high, even_low),
            )
            weave(
                distances(jnp.minimum(n + 2, homes - 1), even_sq, even_cols),
                moments(n, even_high, even_low),
                pairs(n + 1, odd_sq, odd_cols, odd_high, odd_low),
            )
        return carry

    lax.fori_loop(0, homes // 16, turn, 0)
    weave(moments(homes - 1, odd_high, odd_low))


def descreen(dims, mask, type_radius, type_scale, raw, table):
    slots = raw.shape[0]
    smem = pl.BlockSpec(memory_space=pltpu.SMEM)
    vmem = pl.BlockSpec(memory_space=pltpu.VMEM)
    return pl.pallas_call(
        functools.partial(descreen_kernel, dims),
        out_shape=(
            jax.ShapeDtypeStruct((slots, 8, 128), f32),
            jax.ShapeDtypeStruct((slots, 48, 128), bf16),
        ),
        in_specs=[smem, smem, smem, vmem, vmem],
        out_specs=(vmem, vmem),
        scratch_shapes=[
            pltpu.VMEM((slots, 8, 128), f32),
            pltpu.VMEM((128, 13 * 128), f32),
            pltpu.VMEM((128, 13 * 128), f32),
            pltpu.VMEM((6, 128, 128), f32),
            pltpu.VMEM((6, 128, 128), f32),
            pltpu.VMEM((128, 128), f32),
        ],
        compiler_params=pltpu.CompilerParams(vmem_limit_bytes=56 * 2**20),
        name="descreen",
    )(mask, type_radius, type_scale, raw, table)


def screen(dims, mask, raw, born, table, away):
    slots = raw.shape[0]
    smem = pl.BlockSpec(memory_space=pltpu.SMEM)
    vmem = pl.BlockSpec(memory_space=pltpu.VMEM)
    return pl.pallas_call(
        functools.partial(screen_kernel, dims),
        out_shape=(
            jax.ShapeDtypeStruct((slots, 16, 128), f32),
            jax.ShapeDtypeStruct((slots, 16, 128), f32),
        ),
        in_specs=[smem, vmem, vmem, vmem, vmem],
        out_specs=(vmem, vmem),
        scratch_shapes=[
            pltpu.VMEM((slots, 8, 128), f32),
            pltpu.VMEM((slots, 16, 128), bf16),
            pltpu.VMEM((128, 13 * 128), f32),
            pltpu.VMEM((128, 13 * 128), f32),
            pltpu.VMEM((128, 128), f32),
            pltpu.VMEM((128, 128), f32),
            pltpu.VMEM((128, 13 * 128), bf16),
            pltpu.VMEM((128, 13 * 128), bf16),
            pltpu.VMEM((128, 13 * 128), bf16),
            pltpu.VMEM((128, 13 * 128), bf16),
            pltpu.VMEM((2, 128, 128), f32),
        ],
        compiler_params=pltpu.CompilerParams(vmem_limit_bytes=56 * 2**20),
        name="screen",
    )(mask, raw, born, table, away)


def around(dx, dy):
    count_x, count_y = lax.axis_size("gx"), lax.axis_size("gy")
    return (
        lax.rem(lax.axis_index("gx") + (dx + count_x), count_x),
        lax.rem(lax.axis_index("gy") + (dy + count_y), count_y),
    )


def greet():
    barrier = pltpu.get_barrier_semaphore()
    ring = [(dx, dy) for dx in (-1, 0, 1) for dy in (-1, 0, 1) if (dx, dy) != (0, 0)]
    for dx, dy in ring:
        pl.semaphore_signal(barrier, inc=1, device_id=around(dx, dy), device_id_type=pl.DeviceIdType.MESH)


def await_ring():
    pl.semaphore_wait(pltpu.get_barrier_semaphore(), 8)


def send(src, dst, sems, k, to):
    copy = pltpu.make_async_remote_copy(
        src_ref=src,
        dst_ref=dst,
        send_sem=sems.at[0, k],
        recv_sem=sems.at[1, k],
        device_id=around(*to),
        device_id_type=pl.DeviceIdType.MESH,
    )
    copy.start()
    return copy


def fill_halo(ext, sems, rows_x, rows_y):
    own = pl.ds(2, rows_y)
    top, ahead = pl.ds(0, 2), pl.ds(rows_x, 2)
    body_rows = pl.ds(0, rows_x)
    left, first = pl.ds(0, 2), pl.ds(2, 2)
    last, right = pl.ds(rows_y, 2), pl.ds(rows_y + 2, 2)
    plan = [
        (top, own, ahead, own, (-1, 0)),
        (body_rows, last, body_rows, left, (0, 1)),
        (body_rows, first, body_rows, right, (0, -1)),
        (top, last, ahead, left, (-1, 1)),
        (top, first, ahead, right, (-1, -1)),
    ]
    copies = [
        send(ext.at[rs, cs], ext.at[rd, cd], sems, k, to)
        for k, (rs, cs, rd, cd, to) in enumerate(plan)
    ]
    for copy in copies:
        copy.wait()


def give_back(ext, ahead_land, side_land, corner_land, sems, rows_x, rows_y):
    own = pl.ds(2, rows_y)
    ahead, body_rows = pl.ds(rows_x, 2), pl.ds(0, rows_x)
    left, right = pl.ds(0, 2), pl.ds(rows_y + 2, 2)
    copies = [
        send(ext.at[ahead, own], ahead_land, sems, 0, (1, 0)),
        send(ext.at[body_rows, left], side_land.at[0], sems, 1, (0, -1)),
        send(ext.at[body_rows, right], side_land.at[1], sems, 2, (0, 1)),
        send(ext.at[ahead, left], corner_land.at[0], sems, 3, (1, -1)),
        send(ext.at[ahead, right], corner_land.at[1], sems, 4, (1, 1)),
    ]
    for copy in copies:
        copy.wait()
    ext[0:2, 2 : rows_y + 2] += ahead_land[...]
    ext[0:rows_x, rows_y : rows_y + 2] += side_land[0]
    ext[0:rows_x, 2:4] += side_land[1]
    ext[0:2, rows_y : rows_y + 2] += corner_land[0]
    ext[0:2, 2:4] += corner_land[1]


def gather_kernel(radius_ref, scale_ref, offsets_ref, charge_ref, type_ref, ext, sems):
    rows_x, rows_y, _ = charge_ref.shape
    greet()
    for x in range(rows_x):
        for y in range(0, rows_y, 8):
            types = type_ref[x, y : y + 8]
            radius = jnp.zeros((8, 128), f32)
            scale = jnp.zeros((8, 128), f32)
            for k in range(radius_ref.shape[0]):
                radius = jnp.where(types == k, radius_ref[k], radius)
                scale = jnp.where(types == k, scale_ref[k], scale)
            inner = radius - radius_offset
            parts = [offsets_ref[k, x, y : y + 8] for k in range(3)]
            parts += [inner, scale * inner, charge_ref[x, y : y + 8], radius, jnp.zeros((8, 128), f32)]
            for k, part in enumerate(parts):
                ext[x, 2 + y : 10 + y, k, :] = part
    await_ring()
    fill_halo(ext, sems, rows_x, rows_y)


def born_kernel(sum_ref, raw_ref, born_ref, ext, ahead_land, side_land, corner_land, sems):
    width = sum_ref.shape[1]
    rows_x, rows_y = sum_ref.shape[0] - 2, width - 4
    greet()

    def reduce_turn(x, carry):
        for y in range(width):
            ext[x, y] = jnp.sum(sum_ref[x, y], axis=0, keepdims=True)
        return carry

    lax.fori_loop(0, rows_x + 2, reduce_turn, 0)
    await_ring()
    give_back(ext, ahead_land, side_land, corner_land, sems.at[0], rows_x, rows_y)

    def radius_turn(x, carry):
        for y in range(2, rows_y + 2):
            raw = raw_ref[x, y]
            inner, radius = raw[3:4], raw[6:7]
            psi = 0.5 * inner * ext[x, y]
            bent = jnp.tanh(psi * (1.0 - 0.8 * psi + 4.85 * psi * psi))
            born_ref[x, y] = 1.0 / (1.0 / inner - bent / radius)
        return carry

    lax.fori_loop(0, rows_x, radius_turn, 0)
    fill_halo(born_ref, sems.at[1], rows_x, rows_y)


def settle_kernel(
    moment_ref, sum_ref, raw_ref, born_ref, ext, ahead_land, side_land, corner_land, sems
):
    width = sum_ref.shape[1]
    rows_x, rows_y = sum_ref.shape[0] - 2, width - 4
    greet()
    row = sublane()

    def finish_turn(x, carry):
        for y in range(width):
            raw = raw_ref[x, y]
            born = born_ref[x, y]
            inv = 1.0 / born
            weak = raw[5:6] * lax.rsqrt(born)
            strong = weak * inv
            moment = moment_ref[x, y]
            moment = moment[0:8] + moment[8:16]
            moment = moment[0:4] + moment[4:8]
            middle = jnp.where(row == 0, 8.0 * (x.astype(f32) - 0.5 * (rows_x + 1)) - 4.0, 8.0 * (y - 0.5 * (width - 1)) - 4.0)
            place = raw + jnp.where(row == 2, -8.0, middle)
            force = ((-dielectric_factor / 8.0) * strong) * (place[0:3] * moment[0:1] - moment[1:4])
            sums = sum_ref[x, y]
            energy = ((-0.25 * dielectric_factor) * weak) * jnp.sum(sums[0:8], axis=0, keepdims=True)
            grad = ((0.25 * dielectric_factor) * strong) * jnp.sum(sums[8:16], axis=0, keepdims=True)
            ext[x, y] = jnp.concatenate([force, energy, grad, jnp.zeros((3, 128), f32)], axis=0)
        return carry

    lax.fori_loop(0, rows_x + 2, finish_turn, 0)
    await_ring()
    give_back(ext, ahead_land, side_land, corner_land, sems, rows_x, rows_y)


def finish_kernel(ext, raw_ref, born_ref, born_out, energy_out, force_out, grad_out):
    rows_x, rows_y, _ = born_out.shape
    for x in range(rows_x):
        for y in range(0, rows_y, 8):
            here = slice(2 + y, 10 + y)
            there = slice(y, y + 8)
            born = born_ref[x, here, 0, :]
            charge = raw_ref[x, here, 5, :]
            own = (0.5 * dielectric_factor) * (charge * charge) / born
            born_out[x, there] = born
            for k in range(3):
                force_out[k, x, there] = ext[x, here, k, :]
            energy_out[x, there] = ext[x, here, 3, :] - own
            grad_out[x, there] = ext[x, here, 4, :] + own / born


def exchange(kernel, ident, ins, outs, scratch):
    smem = pl.BlockSpec(memory_space=pltpu.SMEM)
    vmem = pl.BlockSpec(memory_space=pltpu.VMEM)
    return pl.pallas_call(
        kernel,
        out_shape=tuple(jax.ShapeDtypeStruct(shape, f32) for shape in outs),
        in_specs=[smem if value.ndim == 1 else vmem for value in ins],
        out_specs=tuple(vmem for _ in outs),
        scratch_shapes=scratch,
        compiler_params=pltpu.CompilerParams(
            collective_id=ident, has_side_effects=ident is not None, vmem_limit_bytes=56 * 2**20
        ),
        name=kernel.__name__,
    )(*ins)


def landing(rows_x, rows_y, depth):
    return [
        pltpu.VMEM((rows_x + 2, rows_y + 4, depth, 128), f32),
        pltpu.VMEM((2, rows_y, depth, 128), f32),
        pltpu.VMEM((2, rows_x, 2, depth, 128), f32),
        pltpu.VMEM((2, 2, 2, depth, 128), f32),
    ]


def body(offsets, charges, atom_type, type_radius, type_scale, tile_mask):
    rows_x, rows_y, atoms = charges.shape
    dims = (rows_x, rows_y)
    grid = (rows_x + 2, rows_y + 4)
    slots = grid[0] * grid[1]
    dma = pltpu.SemaphoreType.DMA
    (raw,) = exchange(
        gather_kernel, 0, (type_radius, type_scale, offsets, charges, atom_type),
        [grid + (8, atoms)], [dma((2, 5))],
    )
    mask = tile_mask.reshape(-1)
    table = step_tables()
    raw_slots = raw.reshape(slots, 8, atoms)
    sums, away = descreen(dims, mask, type_radius, type_scale, raw_slots, table)
    (born,) = exchange(
        born_kernel, 1, (sums.reshape(grid + (8, atoms)), raw),
        [grid + (1, atoms)], landing(rows_x, rows_y, 1) + [dma((2, 2, 5))],
    )
    moments, pair_sums = screen(dims, mask, raw_slots, born.reshape(slots, 1, atoms), table, away)
    (settled,) = exchange(
        settle_kernel, 2,
        (moments.reshape(grid + (16, atoms)), pair_sums.reshape(grid + (16, atoms)), raw, born),
        [grid + (8, atoms)], landing(rows_x, rows_y, 8)[1:] + [dma((2, 5))],
    )
    shape = (rows_x, rows_y, atoms)
    return exchange(
        finish_kernel, None, (settled, raw, born), [shape, shape, (3,) + shape, shape], []
    )


def solution(mesh):
    placed = (
        P(None, "gx", "gy", None),
        P("gx", "gy", None),
        P("gx", "gy", None),
        P(),
        P(),
        P("gx", "gy", None),
    )
    return jax.shard_map(
        body,
        mesh=mesh,
        in_specs=placed,
        out_specs=(
            P("gx", "gy", None),
            P("gx", "gy", None),
            P(None, "gx", "gy", None),
            P("gx", "gy", None),
        ),
        check_vma=False,
    )
```
